32 devices in a mesh: frame: 8 (over z, x), space: 4 (over y, core).
Axes of the slice: x: 2, y: 2, z: 4, core: 2. Of those that a mesh axis runs over, the one named last changes fastest.
Arguments:
- queries: bfloat16 [32, 512, 2240], P('frame', 'space'), may hold values from -6 to 6
- keys: bfloat16 [32, 512, 2240], P('frame', 'space'), may hold values from -16 to 16
- values: bfloat16 [32, 512, 2240], P('frame', 'space'), may hold values from -16 to 16
- out_weight: bfloat16 [2240, 2240], P('frame'), may hold values from -0.125 to 0.125
- conv_taps: float32 [3, 2240], replicated, may hold values from -3 to 3
Outputs:
- mixed: bfloat16 [32, 512, 2240], P('frame', 'space')
The draws below stay inside these ranges and needn't reach their ends.
All inputs are finite; a program needn't handle non-finite values.
Results may differ from the reference program's by a relative error of at most 0.0059.
Values may be sent and summed in bfloat16 or wider, within the bound.
A program may use at most 192 MiB of HBM per device.

```python
import math
import jax
import jax.numpy as jnp
from jax import lax

HEADS = 20
HEAD_DIM = 112
D = 2240
FRAMES = 32
SPATIAL = 512


def key_value_draw(base_key):
    subkeys = jax.random.split(jax.random.fold_in(base_key, 17), 9)
    low_scale = 0.3
    high_scale = 2.0
    token_scale = jnp.exp(jax.random.uniform(subkeys[0], (FRAMES, SPATIAL, 1), jnp.float32, math.log(low_scale), math.log(high_scale)))
    head_gain = jnp.exp(jax.random.uniform(subkeys[5], (1, 1, HEADS, 1), jnp.float32, math.log(0.6), math.log(1.6)))
    channel_gain = jnp.exp(jax.random.uniform(subkeys[6], (1, 1, HEADS, HEAD_DIM), jnp.float32, math.log(0.3), math.log(3.0)))
    frame_channel_gain = jnp.exp(jax.random.uniform(subkeys[7], (FRAMES, 1, HEADS, HEAD_DIM), jnp.float32, math.log(0.6), math.log(1.6)))
    key_gains = (head_gain * channel_gain * frame_channel_gain).reshape(FRAMES, 1, D)
    raw_keys = jax.random.normal(subkeys[1], (FRAMES, SPATIAL, D), jnp.float32) * token_scale * key_gains
    keys_out = jnp.clip(raw_keys, -16.0, 16.0)
    common_mixing = jax.random.normal(subkeys[2], (1, HEADS, HEAD_DIM, HEAD_DIM), jnp.float32) * (0.35 / math.sqrt(HEAD_DIM))
    frame_mixing = jax.random.normal(subkeys[8], (FRAMES, HEADS, HEAD_DIM, HEAD_DIM), jnp.float32) / math.sqrt(HEAD_DIM)
    mixing = common_mixing + frame_mixing
    frame_gain = jnp.exp(jax.random.uniform(subkeys[3], (FRAMES, 1, 1, 1), jnp.float32, math.log(0.3), math.log(3.0)))
    key_relu = jax.nn.relu(keys_out).reshape(FRAMES, SPATIAL, HEADS, HEAD_DIM)
    signal = jnp.einsum('fshd,fhde->fshe', key_relu, mixing, precision=lax.Precision.HIGHEST) * frame_gain
    noise = 0.5 * jax.random.normal(subkeys[4], (FRAMES, SPATIAL, D), jnp.float32)
    values_out = jnp.clip(signal.reshape(FRAMES, SPATIAL, D) + noise, -16.0, 16.0)
    return (keys_out, values_out)


def draw_keys(key, part):
    return key_value_draw(key)[0].astype(jnp.bfloat16)


def draw_values(key, part):
    return key_value_draw(key)[1].astype(jnp.bfloat16)


def level_of(own_key, extent, pieces, least, high):
    def one(axis_at, parts):
        draws = jax.random.uniform(jax.random.fold_in(jax.random.fold_in(own_key, 6), axis_at), (parts,), jnp.float32, least / len(pieces), high / len(pieces))
        return jnp.repeat(jnp.exp(draws), extent[axis_at] // parts).reshape((-1,) + (1,) * (len(extent) - axis_at - 1))

    loudness = one(*pieces[0])
    for cut in pieces[1:]:
        loudness = loudness * one(*cut)
    return loudness


def scatter_about(key, shape, deviation, bound, cuts=(), kind=jnp.bfloat16):
    result = jax.random.normal(key, shape, jnp.float32) * deviation
    if len(cuts) > 0:
        result = level_of(key, shape, cuts, -0.22, 0.18) * result
    return jnp.clip(result, min=-bound, max=bound).astype(kind)


def setup_inputs(seed: int = 0) -> dict:
    key_of = jax.random.split(jax.random.key(seed), 6)
    return {
        "queries": scatter_about(key_of[0], (FRAMES, SPATIAL, D), 1.0, 6.0, ((0, 8), (1, 4))),
        "keys": draw_keys(jax.random.fold_in(key_of[5], 71), 0),
        "values": draw_values(jax.random.fold_in(key_of[5], 71), 0),
        "out_weight": scatter_about(key_of[3], (D, D), D ** -0.5, 0.125, ((0, 8),)),
        "conv_taps": scatter_about(key_of[4], (3, D), 0.6, 3.0, (), jnp.float32),
    }


stab_eps = 1e-6


def reference(queries, keys, values, out_weight, conv_taps):
    frame_count = queries.shape[0]
    spatial_count = queries.shape[1]
    key_relu = jax.nn.relu(keys.astype(jnp.float32)).reshape(frame_count, spatial_count, HEADS, HEAD_DIM)
    value_rows = values.astype(jnp.float32).reshape(frame_count, spatial_count, HEADS, HEAD_DIM)
    frame_kv = jnp.einsum("fshd,fshe->fhde", key_relu, value_rows, precision=lax.Precision.HIGHEST)
    frame_ksum = jnp.sum(key_relu, axis=1)
    states = jnp.cumsum(frame_kv, axis=0)
    norms = jnp.cumsum(frame_ksum, axis=0)
    query_relu = jax.nn.relu(queries.astype(jnp.float32)).reshape(frame_count, spatial_count, HEADS, HEAD_DIM)
    numerator = jnp.einsum("fshd,fhde->fshe", query_relu, states, precision=lax.Precision.HIGHEST)
    denominator = jnp.einsum("fshd,fhd->fsh", query_relu, norms, precision=lax.Precision.HIGHEST) + stab_eps
    attention = (numerator / denominator[..., None]).reshape(frame_count * spatial_count, D).astype(jnp.bfloat16)
    projected = jnp.dot(attention, out_weight, preferred_element_type=jnp.float32).astype(jnp.bfloat16)
    projected = projected.reshape(frame_count, spatial_count, D)
    zero_frame = jnp.zeros((1, spatial_count, D), jnp.bfloat16)
    lag_one = jnp.concatenate([zero_frame, projected[:-1]], axis=0)
    lag_two = jnp.concatenate([zero_frame, zero_frame, projected[:-2]], axis=0)
    mixed = conv_taps[0] * projected + conv_taps[1] * lag_one + conv_taps[2] * lag_two
    return mixed.astype(jnp.bfloat16)
```

```python
import functools

import jax
import jax.numpy as jnp
from jax import lax
from jax.experimental import pallas as pl
from jax.experimental.pallas import tpu as pltpu
from jax.sharding import PartitionSpec as P

HEADS = 20
HEAD_DIM = 112
LANES = 128
HALO = 2
stab_eps = 1e-06
MESH = pl.DeviceIdType.MESH


def exchange(outer, lanes_y, kv_in, w_in, q_in, st_out, w_out, q_out,
             sib_kv, chip_kv, y_kv, frame_kv, x_got, pair_msg, edge_msg, pair_got, edge_got,
             own_sem, kv_sem, z_sem, x_sem, y_sem, sz_sem, sx_sem, sy_sem, p_sem):
    frame = lax.axis_index("frame")
    space = lax.axis_index("space")
    o, i = frame // 2, frame % 2
    y, c = space // 2, space % 2
    frames = kv_in.shape[2]
    rows = w_in.shape[1]
    part = rows // lanes_y

    def at(o_=None, i_=None, y_=None, c_=None):
        o_ = o if o_ is None else o_
        i_ = i if i_ is None else i_
        y_ = y if y_ is None else y_
        c_ = c if c_ is None else c_
        return (o_ * 2 + i_, y_ * 2 + c_)

    def copy(src, dst, sems, to):
        return pltpu.make_async_remote_copy(
            src_ref=src, dst_ref=dst, send_sem=sems.at[0], recv_sem=sems.at[1],
            device_id=to, device_id_type=MESH)

    def when(cond, do):
        if cond is True:
            do()
        else:
            pl.when(cond)(do)

    def y_far(d):
        return lax.rem(y + d, lanes_y)

    def y_from(d):
        return lax.rem(y + lanes_y - d, lanes_y)

    barrier = pltpu.get_barrier_semaphore()

    def greet(to):
        pl.semaphore_signal(barrier, inc=1, device_id=to, device_id_type=MESH)

    for d in range(1, outer):
        greet(at(o_=lax.rem(o + d, outer)))
    for d in range(1, lanes_y):
        greet(at(y_=y_far(d)))
    greet(at(i_=1 - i))
    greet(at(c_=1 - c))
    into = jnp.logical_and(i == 0, o > 0)
    onto = jnp.logical_and(i == 1, o < outer - 1)
    when(into, lambda: greet(at(o_=o - 1, i_=1)))
    when(onto, lambda: greet(at(o_=o + 1, i_=0)))
    peers = (outer - 1) + (lanes_y - 1) + 2
    pl.semaphore_wait(barrier, peers + jnp.where(jnp.logical_or(into, onto), 1, 0))

    def source(key):
        t = (key + 1) // 2
        if key == 0:
            return o, True
        if key % 2:
            return o - t, o >= t
        return o + t, o + t < outer

    keys = range(2 * outer - 1)
    sent = []

    def launch(cond, make):
        when(cond, lambda: make().start())
        sent.append((cond, make))

    def mine(key):
        return w_out.at[c, source(key)[0] * 2 + i]

    def theirs(key, y_):
        span = pl.ds(pl.multiple_of(y_ * part, 16), part)
        return w_out.at[c, source(key)[0] * 2 + 1 - i, span]

    def z_copy(up, t):
        g = ((o - t + 1) if up else (o + t - 1)) * 2 + i
        dst = w_out.at[c, g]
        return copy(w_in.at[c] if t == 1 else dst, dst, z_sem.at[0 if up else 1, t],
                    at(o_=o + 1 if up else o - 1))

    def z_send(t):
        launch(jnp.logical_and(o < outer - 1, o - t + 1 >= 0), lambda: z_copy(True, t))
        launch(jnp.logical_and(o > 0, o + t - 1 < outer), lambda: z_copy(False, t))

    def z_wait(t):
        def got(key, up):
            ref = mine(key)
            copy(ref, ref, z_sem.at[0 if up else 1, t], at(c_=1 - c)).wait_recv()
        when(source(2 * t - 1)[1], lambda: got(2 * t - 1, True))
        when(source(2 * t)[1], lambda: got(2 * t, False))

    def x_copy(key):
        span = pl.ds(pl.multiple_of(y * part, 16), part)
        src = w_in.at[c, span] if key == 0 else mine(key).at[span]
        return copy(src, mine(key).at[span], x_sem.at[key], at(i_=1 - i))

    def x_send(key):
        launch(source(key)[1], lambda: x_copy(key))

    def sib_z(key):
        launch(source(key)[1], lambda: copy(mine(key), mine(key), sz_sem.at[key], at(c_=1 - c)))

    def x_pass(key):
        def got():
            ref = theirs(key, y)
            copy(ref, ref, x_sem.at[key], at(i_=1 - i)).wait_recv()
        cond = source(key)[1]
        when(cond, got)
        for d in range(1, lanes_y):
            launch(cond, lambda d=d: copy(theirs(key, y), theirs(key, y), y_sem.at[key, d],
                                          at(y_=y_far(d))))
        launch(cond, lambda: copy(theirs(key, y), theirs(key, y), sx_sem.at[key], at(c_=1 - c)))

    def y_pass(key):
        cond = source(key)[1]
        for d in range(1, lanes_y):
            def got(d=d):
                ref = theirs(key, y_from(d))
                copy(ref, ref, y_sem.at[key, d], at(y_=y_far(d))).wait_recv()
            when(cond, got)
            launch(cond, lambda d=d: copy(theirs(key, y_from(d)), theirs(key, y_from(d)),
                                          sy_sem.at[key, d], at(c_=1 - c)))

    def sib_wait(key):
        cond = source(key)[1]
        g = source(key)[0] * 2

        def got(ref, sems):
            copy(ref, ref, sems, at(c_=1 - c)).wait_recv()
        if key:
            when(cond, lambda: got(w_out.at[1 - c, g + i], sz_sem.at[key]))
        for d in range(lanes_y):
            span = pl.ds(pl.multiple_of(y_from(d) * part, 16), part)
            sems = sx_sem.at[key] if d == 0 else sy_sem.at[key, d]
            when(cond, lambda span=span, sems=sems: got(w_out.at[1 - c, g + 1 - i, span], sems))

    sib_copy = copy(kv_in.at[1 - c], sib_kv, kv_sem.at[0], at(c_=1 - c))
    sib_copy.start()
    z_send(1)
    x_send(0)
    own = pltpu.make_async_copy(w_in, w_out.at[:, frame], own_sem.at[0])
    own.start()
    last = q_in.at[pl.ds(frames - HALO, HALO)]
    q_next = lambda: copy(last, q_out, p_sem.at[0], (frame + 1, space))
    launch(frame < 2 * outer - 1, q_next)

    sib_copy.wait_recv()
    for y_ in range(lanes_y):
        for f in range(frames):
            chip_kv[y_, f] = (kv_in[c, y_, f].astype(jnp.float32)
                              + sib_kv[y_, f].astype(jnp.float32)).astype(jnp.bfloat16)
    for d in range(1, lanes_y):
        launch(True, lambda d=d: copy(chip_kv.at[y_far(d)], y_kv.at[d], kv_sem.at[1 + d],
                                      at(y_=y_far(d))))
    x_pass(0)
    for d in range(1, lanes_y):
        copy(chip_kv.at[y_far(d)], y_kv.at[d], kv_sem.at[1 + d], at(y_=y_far(d))).wait_recv()
    for f in range(frames):
        total = chip_kv[y, f].astype(jnp.float32)
        for d in range(1, lanes_y):
            total = total + y_kv[d, f].astype(jnp.float32)
        frame_kv[f] = total if f == 0 else frame_kv[f - 1] + total
    for f in range(HALO):
        x_got[0, f] = frame_kv[frames - 1 - f].astype(jnp.bfloat16)
    launch(True, lambda: copy(x_got.at[0], x_got.at[1], p_sem.at[1], at(i_=1 - i)))

    z_wait(1)
    if outer > 2:
        z_send(2)
    for key in (1, 2):
        x_send(key)
        sib_z(key)

    copy(x_got.at[0], x_got.at[1], p_sem.at[1], at(i_=1 - i)).wait_recv()
    pair_msg[...] = (x_got[0, 0].astype(jnp.float32) + x_got[1, 0].astype(jnp.float32)).astype(jnp.bfloat16)
    low = jnp.where(i == 0, x_got[0, 0], x_got[1, 0]).astype(jnp.float32)
    high = jnp.where(i == 0, x_got[1, 1], x_got[0, 1]).astype(jnp.float32)
    edge_msg[...] = (low + high).astype(jnp.bfloat16)
    for d in range(1, outer):
        launch(o + d < outer, lambda d=d: copy(pair_msg, pair_got.at[d], p_sem.at[3 + d], at(o_=o + d)))
    launch(o + 1 < outer, lambda: copy(edge_msg, edge_got, p_sem.at[2], at(o_=o + 1)))

    y_pass(0)
    for key in (1, 2):
        x_pass(key)

    for d in range(1, outer):
        when(o >= d, lambda d=d: copy(pair_msg, pair_got.at[d], p_sem.at[3 + d], at(c_=1 - c)).wait_recv())
    when(o >= 1, lambda: copy(edge_msg, edge_got, p_sem.at[2], at(c_=1 - c)).wait_recv())
    zero = jnp.zeros(pair_msg.shape, jnp.float32)
    far = zero
    for d in range(2, outer):
        far = far + jnp.where(o >= d, pair_got[d].astype(jnp.float32), zero)
    near = jnp.where(o >= 1, pair_got[1].astype(jnp.float32), zero)
    edge = jnp.where(o >= 1, edge_got[...].astype(jnp.float32), zero)
    base = far + near
    before = jnp.where(i == 0, base, base + x_got[1, 0].astype(jnp.float32))
    second = jnp.where(i == 0, far + edge, base + x_got[1, 1].astype(jnp.float32))
    st_out[c, y, 0] = second.astype(jnp.bfloat16)
    st_out[c, y, 1] = before.astype(jnp.bfloat16)
    for f in range(frames):
        st_out[c, y, HALO + f] = (before + frame_kv[f]).astype(jnp.bfloat16)
    for d in range(1, lanes_y):
        launch(True, lambda d=d: copy(st_out.at[c, y], st_out.at[c, y], kv_sem.at[lanes_y + d],
                                      at(y_=y_far(d))))

    for t in range(2, outer):
        z_wait(t)
        if t + 1 < outer:
            z_send(t + 1)
        for key in (2 * t - 1, 2 * t):
            x_send(key)
            sib_z(key)
        for key in (2 * t - 3, 2 * t - 2):
            y_pass(key)
        if t == 2:
            for d in range(1, lanes_y):
                ref = st_out.at[c, y_from(d)]
                copy(ref, ref, kv_sem.at[lanes_y + d], at(y_=y_far(d))).wait_recv()
            launch(True, lambda: copy(st_out.at[c], st_out.at[c], kv_sem.at[1], at(c_=1 - c)))
        for key in (2 * t - 1, 2 * t):
            x_pass(key)
    for key in (2 * outer - 3, 2 * outer - 2):
        y_pass(key)

    other = st_out.at[1 - c]
    copy(other, other, kv_sem.at[1], at(c_=1 - c)).wait_recv()
    when(frame > 0, lambda: copy(last, q_out, p_sem.at[0], at(c_=1 - c)).wait_recv())
    for key in keys:
        sib_wait(key)
    own.wait()
    sib_copy.wait_send()
    for cond, make in sent:
        when(cond, lambda make=make: make().wait_send())


def exchanged(kv, weight, queries, outer, lanes_y):
    rows = kv.shape[3]
    frames = kv.shape[2]
    keys = 2 * outer - 1
    tile = (rows, LANES)
    half = jnp.bfloat16
    dma = pltpu.SemaphoreType.DMA
    whole = pl.BlockSpec(memory_space=pltpu.VMEM)
    anywhere = pl.BlockSpec(memory_space=pl.ANY)
    return pl.pallas_call(
        functools.partial(exchange, outer, lanes_y),
        out_shape=(
            jax.ShapeDtypeStruct((2, lanes_y, HALO + frames) + tile, half),
            jax.ShapeDtypeStruct((2, 2 * outer) + weight.shape[1:], half),
            jax.ShapeDtypeStruct((HALO,) + queries.shape[1:], half),
        ),
        in_specs=[whole, anywhere, anywhere],
        out_specs=(whole, anywhere, anywhere),
        scratch_shapes=[
            pltpu.VMEM((lanes_y, frames) + tile, half),
            pltpu.VMEM((lanes_y, frames) + tile, half),
            pltpu.VMEM((lanes_y, frames) + tile, half),
            pltpu.VMEM((frames,) + tile, jnp.float32),
            pltpu.VMEM((2, HALO) + tile, half),
            pltpu.VMEM(tile, half),
            pltpu.VMEM(tile, half),
            pltpu.VMEM((outer,) + tile, half),
            pltpu.VMEM(tile, half),
            dma((1,)),
            dma((2 * lanes_y, 2)),
            dma((2, outer, 2)),
            dma((keys, 2)),
            dma((keys, lanes_y, 2)),
            dma((keys, 2)),
            dma((keys, 2)),
            dma((keys, lanes_y, 2)),
            dma((3 + outer, 2)),
        ],
        compiler_params=pltpu.CompilerParams(
            collective_id=0, has_side_effects=True, vmem_limit_bytes=40 * 2**20),
    )(kv, weight, queries)


def up_to(value, multiple):
    return -(-value // multiple) * multiple


def per_device(sections, lanes, queries, keys, values, out_weight, conv_taps):
    frames, tokens, width = queries.shape
    lanes_y = lanes // 2
    outer = sections // 2
    key_relu = jax.nn.relu(keys).reshape(frames, tokens, HEADS, HEAD_DIM)
    rows = values.reshape(frames, tokens, HEADS, HEAD_DIM)
    ones = jnp.ones((frames, tokens, HEADS, 1), rows.dtype)
    rows = jnp.pad(jnp.concatenate([rows, ones], axis=3), ((0, 0), (0, 0), (0, 0), (0, LANES - HEAD_DIM - 1)))
    kv = jnp.einsum("fshd,fshe->fhde", key_relu, rows, preferred_element_type=jnp.float32)
    kv = kv.astype(jnp.bfloat16).reshape(frames, width, LANES)
    tall = up_to(width, 16 * lanes)
    kv = jnp.pad(kv, ((0, 0), (0, tall - width), (0, 0)))
    kv = kv.reshape(frames, 2, lanes_y, tall // lanes, LANES).transpose(1, 2, 0, 3, 4)
    deep = out_weight.shape[0]
    deep_pad = up_to(deep, 16 * lanes_y)
    wide = up_to(width, 2 * LANES)
    weight = jnp.pad(out_weight, ((0, deep_pad - deep), (0, wide - width)))
    weight = weight.reshape(deep_pad, 2, wide // 2).transpose(1, 0, 2)
    states, weight, earlier = exchanged(kv, weight, queries, outer, lanes_y)
    states = states.transpose(2, 0, 1, 3, 4).reshape(HALO + frames, tall, LANES)[:, :width]
    states = states.reshape(HALO + frames, HEADS, HEAD_DIM, LANES)
    first = lax.axis_index("frame") == 0
    earlier = jnp.where(first, jnp.zeros_like(earlier), earlier)
    query_relu = jax.nn.relu(jnp.concatenate([earlier, queries], axis=0))
    query_relu = query_relu.reshape(HALO + frames, tokens, HEADS, HEAD_DIM)
    sums = jnp.einsum("fshd,fhde->fshe", query_relu, states, preferred_element_type=jnp.float32)
    attention = sums[..., :HEAD_DIM] / (sums[..., HEAD_DIM:HEAD_DIM + 1] + stab_eps)
    attention = attention.astype(jnp.bfloat16).reshape((HALO + frames) * tokens, sections, deep)
    attention = jnp.pad(attention, ((0, 0), (0, 0), (0, deep_pad - deep)))
    attention = attention.reshape((HALO + frames) * tokens, sections * deep_pad)
    weight = weight.reshape(2, sections * deep_pad, wide // 2)
    projected = jnp.concatenate(
        [jnp.dot(attention, weight[n], preferred_element_type=jnp.float32).astype(jnp.bfloat16)
         for n in range(2)], axis=1)[:, :width]
    extended = projected.reshape(HALO + frames, tokens, width)
    mixed = conv_taps[0] * extended[2:] + conv_taps[1] * extended[1:-1] + conv_taps[2] * extended[:-2]
    return mixed.astype(jnp.bfloat16)


def solution(mesh):
    split = P("frame", "space", None)
    return jax.shard_map(
        functools.partial(per_device, mesh.shape["frame"], mesh.shape["space"]), mesh=mesh,
        in_specs=(split, split, split, P("frame", None), P()), out_specs=split, check_vma=False)
```

```python
import functools

import jax
import jax.numpy as jnp
from jax import lax
from jax.experimental import pallas as pl
from jax.experimental.pallas import tpu as pltpu
from jax.sharding import PartitionSpec as P

HEADS = 20
HEAD_DIM = 112
LANES = 128
HALO = 2
stab_eps = 1e-06
MESH = pl.DeviceIdType.MESH


def exchange(outer, lanes_y, kv_in, w_in, q_in, st_out, w_out, q_out,
             sib_kv, chip_kv, y_kv, frame_kv, x_got, pair_msg, edge_msg, pair_got, edge_got,
             own_sem, kv_sem, z_sem, x_sem, y_sem, sz_sem, sx_sem, sy_sem, p_sem):
    frame = lax.axis_index("frame")
    space = lax.axis_index("space")
    o, i = frame // 2, frame % 2
    y, c = space // 2, space % 2
    frames = kv_in.shape[2]
    rows = w_in.shape[1]
    part = rows // lanes_y

    def at(o_=None, i_=None, y_=None, c_=None):
        o_ = o if o_ is None else o_
        i_ = i if i_ is None else i_
        y_ = y if y_ is None else y_
        c_ = c if c_ is None else c_
        return (o_ * 2 + i_, y_ * 2 + c_)

    def copy(src, dst, sems, to):
        return pltpu.make_async_remote_copy(
            src_ref=src, dst_ref=dst, send_sem=sems.at[0], recv_sem=sems.at[1],
            device_id=to, device_id_type=MESH)

    def when(cond, do):
        if cond is True:
            do()
        else:
            pl.when(cond)(do)

    def y_far(d):
        return lax.rem(y + d, lanes_y)

    def y_from(d):
        return lax.rem(y + lanes_y - d, lanes_y)

    barrier = pltpu.get_barrier_semaphore()

    def greet(to):
        pl.semaphore_signal(barrier, inc=1, device_id=to, device_id_type=MESH)

    for d in range(1, outer):
        greet(at(o_=lax.rem(o + d, outer)))
    for d in range(1, lanes_y):
        greet(at(y_=y_far(d)))
    greet(at(i_=1 - i))
    greet(at(c_=1 - c))
    into = jnp.logical_and(i == 0, o > 0)
    onto = jnp.logical_and(i == 1, o < outer - 1)
    when(into, lambda: greet(at(o_=o - 1, i_=1)))
    when(onto, lambda: greet(at(o_=o + 1, i_=0)))
    peers = (outer - 1) + (lanes_y - 1) + 2
    pl.semaphore_wait(barrier, peers + jnp.where(jnp.logical_or(into, onto), 1, 0))

    def source(key):
        t = (key + 1) // 2
        if key == 0:
            return o, True
        if key % 2:
            return o - t, o >= t
        return o + t, o + t < outer

    keys = range(2 * outer - 1)
    sent = []

    def launch(cond, make):
        when(cond, lambda: make().start())
        sent.append((cond, make))

    def mine(key):
        return w_out.at[c, source(key)[0] * 2 + i]

    def theirs(key, y_):
        span = pl.ds(pl.multiple_of(y_ * part, 16), part)
        return w_out.at[c, source(key)[0] * 2 + 1 - i, span]

    def z_copy(up, t):
        g = ((o - t + 1) if up else (o + t - 1)) * 2 + i
        dst = w_out.at[c, g]
        return copy(w_in.at[c] if t == 1 else dst, dst, z_sem.at[0 if up else 1, t],
                    at(o_=o + 1 if up else o - 1))

    def z_send(t):
        launch(jnp.logical_and(o < outer - 1, o - t + 1 >= 0), lambda: z_copy(True, t))
        launch(jnp.logical_and(o > 0, o + t - 1 < outer), lambda: z_copy(False, t))

    def z_wait(t):
        def got(key, up):
            ref = mine(key)
            copy(ref, ref, z_sem.at[0 if up else 1, t], at(c_=1 - c)).wait_recv()
        when(source(2 * t - 1)[1], lambda: got(2 * t - 1, True))
        when(source(2 * t)[1], lambda: got(2 * t, False))

    def x_copy(key):
        span = pl.ds(pl.multiple_of(y * part, 16), part)
        src = w_in.at[c, span] if key == 0 else mine(key).at[span]
        return copy(src, mine(key).at[span], x_sem.at[key], at(i_=1 - i))

    def x_send(key):
        launch(source(key)[1], lambda: x_copy(key))

    def sib_z(key):
        launch(source(key)[1], lambda: copy(mine(key), mine(key), sz_sem.at[key], at(c_=1 - c)))

    def x_pass(key):
        def got():
            ref = theirs(key, y)
            copy(ref, ref, x_sem.at[key], at(i_=1 - i)).wait_recv()
        cond = source(key)[1]
        when(cond, got)
        for d in range(1, lanes_y):
            launch(cond, lambda d=d: copy(theirs(key, y), theirs(key, y), y_sem.at[key, d],
                                          at(y_=y_far(d))))
        launch(cond, lambda: copy(theirs(key, y), theirs(key, y), sx_sem.at[key], at(c_=1 - c)))

    def y_pass(key):
        cond = source(key)[1]
        for d in range(1, lanes_y):
            def got(d=d):
                ref = theirs(key, y_from(d))
                copy(ref, ref, y_sem.at[key, d], at(y_=y_far(d))).wait_recv()
            when(cond, got)
            launch(cond, lambda d=d: copy(theirs(key, y_from(d)), theirs(key, y_from(d)),
                                          sy_sem.at[key, d], at(c_=1 - c)))

    def sib_wait(key):
        cond = source(key)[1]
        g = source(key)[0] * 2

        def got(ref, sems):
            copy(ref, ref, sems, at(c_=1 - c)).wait_recv()
        if key:
            when(cond, lambda: got(w_out.at[1 - c, g + i], sz_sem.at[key]))
        for d in range(lanes_y):
            span = pl.ds(pl.multiple_of(y_from(d) * part, 16), part)
            sems = sx_sem.at[key] if d == 0 else sy_sem.at[key, d]
            when(cond, lambda span=span, sems=sems: got(w_out.at[1 - c, g + 1 - i, span], sems))

    sib_copy = copy(kv_in.at[1 - c], sib_kv, kv_sem.at[0], at(c_=1 - c))
    sib_copy.start()
    z_send(1)
    x_send(0)
    own = pltpu.make_async_copy(w_in, w_out.at[:, frame], own_sem.at[0])
    own.start()
    last = q_in.at[pl.ds(frames - HALO, HALO)]
    q_next = lambda: copy(last, q_out, p_sem.at[0], (frame + 1, space))
    launch(frame < 2 * outer - 1, q_next)

    sib_copy.wait_recv()
    for y_ in range(lanes_y):
        for f in range(frames):
            chip_kv[y_, f] = (kv_in[c, y_, f].astype(jnp.float32)
                              + sib_kv[y_, f].astype(jnp.float32)).astype(jnp.bfloat16)
    for d in range(1, lanes_y):
        launch(True, lambda d=d: copy(chip_kv.at[y_far(d)], y_kv.at[d], kv_sem.at[1 + d],
                                      at(y_=y_far(d))))
    x_pass(0)
    for d in range(1, lanes_y):
        copy(chip_kv.at[y_far(d)], y_kv.at[d], kv_sem.at[1 + d], at(y_=y_far(d))).wait_recv()
    for f in range(frames):
        total = chip_kv[y, f].astype(jnp.float32)
        for d in range(1, lanes_y):
            total = total + y_kv[d, f].astype(jnp.float32)
        frame_kv[f] = total if f == 0 else frame_kv[f - 1] + total
    for f in range(HALO):
        x_got[0, f] = frame_kv[frames - 1 - f].astype(jnp.bfloat16)
    launch(True, lambda: copy(x_got.at[0], x_got.at[1], p_sem.at[1], at(i_=1 - i)))

    z_wait(1)
    if outer > 2:
        z_send(2)
    for key in (1, 2):
        x_send(key)
        sib_z(key)

    copy(x_got.at[0], x_got.at[1], p_sem.at[1], at(i_=1 - i)).wait_recv()
    pair_msg[...] = (x_got[0, 0].astype(jnp.float32) + x_got[1, 0].astype(jnp.float32)).astype(jnp.bfloat16)
    low = jnp.where(i == 0, x_got[0, 0], x_got[1, 0]).astype(jnp.float32)
    high = jnp.where(i == 0, x_got[1, 1], x_got[0, 1]).astype(jnp.float32)
    edge_msg[...] = (low + high).astype(jnp.bfloat16)
    for d in range(1, outer):
        launch(o + d < outer, lambda d=d: copy(pair_msg, pair_got.at[d], p_sem.at[3 + d], at(o_=o + d)))
    launch(o + 1 < outer, lambda: copy(edge_msg, edge_got, p_sem.at[2], at(o_=o + 1)))

    y_pass(0)
    for key in (1, 2):
        x_pass(key)

    for d in range(1, outer):
        when(o >= d, lambda d=d: copy(pair_msg, pair_got.at[d], p_sem.at[3 + d], at(c_=1 - c)).wait_recv())
    when(o >= 1, lambda: copy(edge_msg, edge_got, p_sem.at[2], at(c_=1 - c)).wait_recv())
    zero = jnp.zeros(pair_msg.shape, jnp.float32)
    far = zero
    for d in range(2, outer):
        far = far + jnp.where(o >= d, pair_got[d].astype(jnp.float32), zero)
    near = jnp.where(o >= 1, pair_got[1].astype(jnp.float32), zero)
    edge = jnp.where(o >= 1, edge_got[...].astype(jnp.float32), zero)
    base = far + near
    before = jnp.where(i == 0, base, base + x_got[1, 0].astype(jnp.float32))
    second = jnp.where(i == 0, far + edge, base + x_got[1, 1].astype(jnp.float32))
    st_out[c, y, 0] = second.astype(jnp.bfloat16)
    st_out[c, y, 1] = before.astype(jnp.bfloat16)
    for f in range(frames):
        st_out[c, y, HALO + f] = (before + frame_kv[f]).astype(jnp.bfloat16)
    for d in range(1, lanes_y):
        launch(True, lambda d=d: copy(st_out.at[c, y], st_out.at[c, y], kv_sem.at[lanes_y + d],
                                      at(y_=y_far(d))))

    for t in range(2, outer):
        z_wait(t)
        if t + 1 < outer:
            z_send(t + 1)
        for key in (2 * t - 1, 2 * t):
            x_send(key)
            sib_z(key)
        for key in (2 * t - 3, 2 * t - 2):
            y_pass(key)
        if t == 2:
            for d in range(1, lanes_y):
                ref = st_out.at[c, y_from(d)]
                copy(ref, ref, kv_sem.at[lanes_y + d], at(y_=y_far(d))).wait_recv()
            launch(True, lambda: copy(st_out.at[c], st_out.at[c], kv_sem.at[1], at(c_=1 - c)))
        for key in (2 * t - 1, 2 * t):
            x_pass(key)
    for key in (2 * outer - 3, 2 * outer - 2):
        y_pass(key)

    other = st_out.at[1 - c]
    copy(other, other, kv_sem.at[1], at(c_=1 - c)).wait_recv()
    when(frame > 0, lambda: copy(last, q_out, p_sem.at[0], at(c_=1 - c)).wait_recv())
    for key in keys:
        sib_wait(key)
    own.wait()
    sib_copy.wait_send()
    for cond, make in sent:
        when(cond, lambda make=make: make().wait_send())


def exchanged(kv, weight, queries, outer, lanes_y):
    rows = kv.shape[3]
    frames = kv.shape[2]
    keys = 2 * outer - 1
    tile = (rows, LANES)
    half = jnp.bfloat16
    dma = pltpu.SemaphoreType.DMA
    whole = pl.BlockSpec(memory_space=pltpu.VMEM)
    anywhere = pl.BlockSpec(memory_space=pl.ANY)
    return pl.pallas_call(
        functools.partial(exchange, outer, lanes_y),
        out_shape=(
            jax.ShapeDtypeStruct((2, lanes_y, HALO + frames) + tile, half),
            jax.ShapeDtypeStruct((2, 2 * outer) + weight.shape[1:], half),
            jax.ShapeDtypeStruct((HALO,) + queries.shape[1:], half),
        ),
        in_specs=[whole, anywhere, anywhere],
        out_specs=(whole, anywhere, anywhere),
        scratch_shapes=[
            pltpu.VMEM((lanes_y, frames) + tile, half),
            pltpu.VMEM((lanes_y, frames) + tile, half),
            pltpu.VMEM((lanes_y, frames) + tile, half),
            pltpu.VMEM((frames,) + tile, jnp.float32),
            pltpu.VMEM((2, HALO) + tile, half),
            pltpu.VMEM(tile, half),
            pltpu.VMEM(tile, half),
            pltpu.VMEM((outer,) + tile, half),
            pltpu.VMEM(tile, half),
            dma((1,)),
            dma((2 * lanes_y, 2)),
            dma((2, outer, 2)),
            dma((keys, 2)),
            dma((keys, lanes_y, 2)),
            dma((keys, 2)),
            dma((keys, 2)),
            dma((keys, lanes_y, 2)),
            dma((3 + outer, 2)),
        ],
        compiler_params=pltpu.CompilerParams(
            collective_id=0, has_side_effects=True, vmem_limit_bytes=40 * 2**20),
    )(kv, weight, queries)


def cuts(start, stop, size):
    while start < stop:
        end = min(stop, (start // size + 1) * size)
        yield start, end
        start = end


def project(deep, q_ref, early_ref, states_ref, w_hbm, taps_ref, out_ref, w_ref, att_ref, w_sem):
    frames, tokens, width = q_ref.shape
    lanes_y, rows = states_ref.shape[1], states_ref.shape[3]
    deep_pad, half = w_hbm.shape[2], w_hbm.shape[3]
    sections = w_hbm.shape[1]
    loads = [pltpu.make_async_copy(w_hbm.at[n], w_ref.at[n], w_sem.at[n]) for n in range(2)]
    for load in loads:
        load.start()

    def attend(f, query):
        span = pl.ds(pl.multiple_of(f * tokens, 16), tokens)
        for h in range(HEADS):
            low, high = h * HEAD_DIM, (h + 1) * HEAD_DIM
            state = [states_ref[(p // rows) // lanes_y, (p // rows) % lanes_y, f, p % rows:p % rows + e - p]
                     for p, e in cuts(low, high, rows)]
            state = state[0] if len(state) == 1 else jnp.concatenate(state, axis=0)
            sums = jnp.dot(query(low, high), state, preferred_element_type=jnp.float32)
            scale = 1.0 / (sums[:, HEAD_DIM:HEAD_DIM + 1] + stab_eps)
            result = (sums * scale).astype(jnp.bfloat16)
            for p, e in cuts(low, high, deep):
                to = p // deep * deep_pad + p % deep
                att_ref[span, to:to + e - p] = result[:, p - low:e - low]

    for n in range(sections):
        att_ref[:, n * deep_pad + deep:(n + 1) * deep_pad] = jnp.zeros(
            (att_ref.shape[0], deep_pad - deep), jnp.bfloat16)

    first = lax.axis_index("frame") == 0

    @pl.when(first)
    def _():
        att_ref[0:HALO * tokens] = jnp.zeros((HALO * tokens, att_ref.shape[1]), jnp.bfloat16)

    @pl.when(jnp.logical_not(first))
    def _():
        @pl.loop(0, HALO)
        def _(f):
            attend(f, lambda low, high: jnp.maximum(early_ref[f, :, low:high], 0))

    @pl.loop(0, frames)
    def _(f):
        attend(f + HALO, lambda low, high: jnp.maximum(q_ref[f, :, low:high], 0))

    def columns(weight, start, count):
        result = jnp.dot(att_ref[...], weight, preferred_element_type=jnp.float32)
        result = result.astype(jnp.bfloat16).astype(jnp.float32)
        result = result.reshape(HALO + frames, tokens, weight.shape[1])[:, :, :count]
        span = pl.ds(start, count)
        mixed = (taps_ref[0:1, span] * result[HALO:] + taps_ref[1:2, span] * result[1:-1]
                 + taps_ref[2:3, span] * result[:-HALO])
        out_ref[:, :, span] = mixed.astype(jnp.bfloat16)

    deepest = sections * deep_pad
    step = 2 * LANES
    whole = half // step
    rest = half - whole * step

    def weight(n, span):
        return w_ref[n, :, :, span].reshape(deepest, span.size)

    loads[0].wait()

    @pl.loop(0, whole)
    def _(t):
        at = pl.multiple_of(t * step, step)
        columns(weight(0, pl.ds(at, step)), at, step)

    loads[1].wait()
    if rest:
        both = jnp.concatenate([weight(0, pl.ds(half - rest, rest)), weight(1, pl.ds(0, rest))], axis=1)
        columns(both, half - rest, 2 * rest)

    @pl.loop(0, whole - 1)
    def _(t):
        at = pl.multiple_of(t * step + rest, LANES)
        columns(weight(1, pl.ds(at, step)), pl.multiple_of(half + at, step), step)

    at = (whole - 1) * step + rest
    columns(weight(1, pl.ds(at, step)), half + at, width - half - at)


def projection(queries, earlier, states, weight, taps, deep):
    frames, tokens, width = queries.shape
    rows = (HALO + frames) * tokens
    depth = weight.shape[1] * weight.shape[2]
    whole = pl.BlockSpec(memory_space=pltpu.VMEM)
    return pl.pallas_call(
        functools.partial(project, deep),
        out_shape=jax.ShapeDtypeStruct(queries.shape, queries.dtype),
        in_specs=[whole, whole, whole, pl.BlockSpec(memory_space=pl.ANY), whole],
        out_specs=whole,
        scratch_shapes=[
            pltpu.VMEM(weight.shape, weight.dtype),
            pltpu.VMEM((rows, depth), jnp.bfloat16),
            pltpu.SemaphoreType.DMA((2,)),
        ],
        cost_estimate=pl.CostEstimate(
            flops=2 * rows * depth * width, bytes_accessed=2 * depth * width, transcendentals=0),
        compiler_params=pltpu.CompilerParams(vmem_limit_bytes=50 * 2**20),
    )(queries, earlier, states, weight, taps)


def up_to(value, multiple):
    return -(-value // multiple) * multiple


def per_device(sections, lanes, queries, keys, values, out_weight, conv_taps):
    frames, tokens, width = queries.shape
    lanes_y = lanes // 2
    outer = sections // 2
    key_relu = jax.nn.relu(keys).reshape(frames, tokens, HEADS, HEAD_DIM)
    rows = values.reshape(frames, tokens, HEADS, HEAD_DIM)
    ones = jnp.ones((frames, tokens, HEADS, 1), rows.dtype)
    rows = jnp.pad(jnp.concatenate([rows, ones], axis=3), ((0, 0), (0, 0), (0, 0), (0, LANES - HEAD_DIM - 1)))
    kv = jnp.einsum("fshd,fshe->fhde", key_relu, rows, preferred_element_type=jnp.float32)
    kv = kv.astype(jnp.bfloat16).reshape(frames, width, LANES)
    tall = up_to(width, 16 * lanes)
    kv = jnp.pad(kv, ((0, 0), (0, tall - width), (0, 0)))
    kv = kv.reshape(frames, 2, lanes_y, tall // lanes, LANES).transpose(1, 2, 0, 3, 4)
    deep = out_weight.shape[0]
    deep_pad = up_to(deep, 16 * lanes_y)
    wide = up_to(width, 2 * LANES)
    weight = jnp.pad(out_weight, ((0, deep_pad - deep), (0, wide - width)))
    weight = weight.reshape(deep_pad, 2, wide // 2).transpose(1, 0, 2)
    states, weight, earlier = exchanged(kv, weight, queries, outer, lanes_y)
    return projection(queries, earlier, states, weight, conv_taps, deep)


def solution(mesh):
    split = P("frame", "space", None)
    return jax.shard_map(
        functools.partial(per_device, mesh.shape["frame"], mesh.shape["space"]), mesh=mesh,
        in_specs=(split, split, split, P("frame", None), P()), out_specs=split, check_vma=False)
```

```python
import functools

import jax
import jax.numpy as jnp
from jax import lax
from jax.experimental import pallas as pl
from jax.experimental.pallas import tpu as pltpu
from jax.sharding import PartitionSpec as P

HEADS = 20
HEAD_DIM = 112
LANES = 128
HALO = 2
stab_eps = 1e-06
MESH = pl.DeviceIdType.MESH


def cuts(start, stop, size):
    while start < stop:
        end = min(stop, (start // size + 1) * size)
        yield start, end
        start = end


def exchange(outer, lanes_y, k_in, v_in, w_in, q_in, cum_out, pre_out, w_out, q_out,
             kv_in, sib_kv, chip_kv, y_kv, frame_kv, cum, pre, x_got, pair_msg, edge_msg, pair_got, edge_got,
             own_sem, kv_sem, z_sem, x_sem, y_sem, sz_sem, sx_sem, sy_sem, p_sem):
    frame = lax.axis_index("frame")
    space = lax.axis_index("space")
    o, i = frame // 2, frame % 2
    y, c = space // 2, space % 2
    frames, tall = kv_in.shape[2], kv_in.shape[3]
    rows = w_in.shape[1]
    part = rows // lanes_y

    def at(o_=None, i_=None, y_=None, c_=None):
        o_ = o if o_ is None else o_
        i_ = i if i_ is None else i_
        y_ = y if y_ is None else y_
        c_ = c if c_ is None else c_
        return (o_ * 2 + i_, y_ * 2 + c_)

    def copy(src, dst, sems, to):
        return pltpu.make_async_remote_copy(
            src_ref=src, dst_ref=dst, send_sem=sems.at[0], recv_sem=sems.at[1],
            device_id=to, device_id_type=MESH)

    def when(cond, do):
        if cond is True:
            do()
        else:
            pl.when(cond)(do)

    def y_far(d):
        return lax.rem(y + d, lanes_y)

    def y_from(d):
        return lax.rem(y + lanes_y - d, lanes_y)

    barrier = pltpu.get_barrier_semaphore()

    def greet(to):
        pl.semaphore_signal(barrier, inc=1, device_id=to, device_id_type=MESH)

    for d in range(1, outer):
        greet(at(o_=lax.rem(o + d, outer)))
    for d in range(1, lanes_y):
        greet(at(y_=y_far(d)))
    greet(at(i_=1 - i))
    greet(at(c_=1 - c))
    into = jnp.logical_and(i == 0, o > 0)
    onto = jnp.logical_and(i == 1, o < outer - 1)
    when(into, lambda: greet(at(o_=o - 1, i_=1)))
    when(onto, lambda: greet(at(o_=o + 1, i_=0)))
    peers = (outer - 1) + (lanes_y - 1) + 2
    pl.semaphore_wait(barrier, peers + jnp.where(jnp.logical_or(into, onto), 1, 0))

    def source(key):
        t = (key + 1) // 2
        if key == 0:
            return o, True
        if key % 2:
            return o - t, o >= t
        return o + t, o + t < outer

    keys = range(2 * outer - 1)
    sent = []

    def launch(cond, make):
        when(cond, lambda: make().start())
        sent.append((cond, make))

    def mine(key):
        return w_out.at[c, source(key)[0] * 2 + i]

    def theirs(key, y_):
        span = pl.ds(pl.multiple_of(y_ * part, 16), part)
        return w_out.at[c, source(key)[0] * 2 + 1 - i, span]

    def z_copy(up, t):
        g = ((o - t + 1) if up else (o + t - 1)) * 2 + i
        dst = w_out.at[c, g]
        return copy(w_in.at[c] if t == 1 else dst, dst, z_sem.at[0 if up else 1, t],
                    at(o_=o + 1 if up else o - 1))

    def z_send(t):
        launch(jnp.logical_and(o < outer - 1, o - t + 1 >= 0), lambda: z_copy(True, t))
        launch(jnp.logical_and(o > 0, o + t - 1 < outer), lambda: z_copy(False, t))

    def z_wait(t):
        def got(key, up):
            ref = mine(key)
            copy(ref, ref, z_sem.at[0 if up else 1, t], at(c_=1 - c)).wait_recv()
        when(source(2 * t - 1)[1], lambda: got(2 * t - 1, True))
        when(source(2 * t)[1], lambda: got(2 * t, False))

    def x_copy(key):
        span = pl.ds(pl.multiple_of(y * part, 16), part)
        src = w_in.at[c, span] if key == 0 else mine(key).at[span]
        return copy(src, mine(key).at[span], x_sem.at[key], at(i_=1 - i))

    def x_send(key):
        launch(source(key)[1], lambda: x_copy(key))

    def sib_z(key):
        launch(source(key)[1], lambda: copy(mine(key), mine(key), sz_sem.at[key], at(c_=1 - c)))

    def x_pass(key):
        def got():
            ref = theirs(key, y)
            copy(ref, ref, x_sem.at[key], at(i_=1 - i)).wait_recv()
        cond = source(key)[1]
        when(cond, got)
        for d in range(1, lanes_y):
            launch(cond, lambda d=d: copy(theirs(key, y), theirs(key, y), y_sem.at[key, d],
                                          at(y_=y_far(d))))
        launch(cond, lambda: copy(theirs(key, y), theirs(key, y), sx_sem.at[key], at(c_=1 - c)))

    def y_pass(key):
        cond = source(key)[1]
        for d in range(1, lanes_y):
            def got(d=d):
                ref = theirs(key, y_from(d))
                copy(ref, ref, y_sem.at[key, d], at(y_=y_far(d))).wait_recv()
            when(cond, got)
            launch(cond, lambda d=d: copy(theirs(key, y_from(d)), theirs(key, y_from(d)),
                                          sy_sem.at[key, d], at(c_=1 - c)))

    def sib_wait(key):
        cond = source(key)[1]
        g = source(key)[0] * 2

        def got(ref, sems):
            copy(ref, ref, sems, at(c_=1 - c)).wait_recv()
        if key:
            when(cond, lambda: got(w_out.at[1 - c, g + i], sz_sem.at[key]))
        for d in range(lanes_y):
            span = pl.ds(pl.multiple_of(y_from(d) * part, 16), part)
            sems = sx_sem.at[key] if d == 0 else sy_sem.at[key, d]
            when(cond, lambda span=span, sems=sems: got(w_out.at[1 - c, g + 1 - i, span], sems))

    z_send(1)
    x_send(0)
    locals_ = [pltpu.make_async_copy(w_in, w_out.at[:, frame], own_sem.at[0])]
    locals_[0].start()

    def halo(f):
        launch(frame < 2 * outer - 1,
               lambda: copy(q_in.at[frames - HALO + f], q_out.at[f], p_sem.at[f], (frame + 1, space)))

    tokens = k_in.shape[2]
    gap = LANES - HEAD_DIM
    nothing = jnp.zeros((gap, tokens), jnp.bfloat16)
    ones = jnp.ones((gap, tokens), jnp.bfloat16)

    @pl.loop(0, frames)
    def _(f):
        for h in range(HEADS):
            span = slice(h * HEAD_DIM, (h + 1) * HEAD_DIM)
            key = jnp.concatenate([jnp.maximum(k_in[f, span], 0), nothing], axis=0)
            value = jnp.concatenate([v_in[f, span], ones], axis=0)
            sums = lax.dot_general(value, key, (((1,), (1,)), ((), ())),
                                   preferred_element_type=jnp.float32).astype(jnp.bfloat16)
            for p, e in cuts(h * LANES, (h + 1) * LANES, tall):
                n = p // tall
                kv_in[n // lanes_y, n % lanes_y, f, p % tall:p % tall + e - p] = (
                    sums[p - h * LANES:e - h * LANES])

    sib_copy = copy(kv_in.at[1 - c], sib_kv, kv_sem.at[0], at(c_=1 - c))
    sib_copy.start()
    sib_copy.wait_recv()
    for d in list(range(1, lanes_y)) + [0]:
        to = y_far(d)
        for f in range(frames):
            chip_kv[to, f] = (kv_in[c, to, f].astype(jnp.float32)
                              + sib_kv[to, f].astype(jnp.float32)).astype(jnp.bfloat16)
        if d:
            launch(True, lambda d=d: copy(chip_kv.at[y_far(d)], y_kv.at[d], kv_sem.at[3 + d],
                                          at(y_=y_far(d))))
    halo(0)
    z_wait(1)
    if outer > 2:
        z_send(2)
    for key in (1, 2):
        x_send(key)
        sib_z(key)
    for d in range(1, lanes_y):
        copy(chip_kv.at[y_far(d)], y_kv.at[d], kv_sem.at[3 + d], at(y_=y_far(d))).wait_recv()
    for f in range(frames):
        total = chip_kv[y, f].astype(jnp.float32)
        for d in range(1, lanes_y):
            total = total + y_kv[d, f].astype(jnp.float32)
        frame_kv[f] = total if f == 0 else frame_kv[f - 1] + total
    for f in range(HALO):
        x_got[0, f] = frame_kv[frames - 1 - f].astype(jnp.bfloat16)
    launch(True, lambda: copy(x_got.at[0], x_got.at[1], p_sem.at[HALO], at(i_=1 - i)))
    for f in range(frames):
        cum[f] = frame_kv[f].astype(jnp.bfloat16)
    for d in range(1, lanes_y):
        launch(True, lambda d=d: copy(cum, cum_out.at[c, y], kv_sem.at[3 + lanes_y + d], at(y_=y_far(d))))
    locals_.append(pltpu.make_async_copy(cum, cum_out.at[c, y], own_sem.at[1]))
    locals_[1].start()
    x_pass(0)

    def pair():
        copy(x_got.at[0], x_got.at[1], p_sem.at[HALO], at(i_=1 - i)).wait_recv()
        pair_msg[...] = (x_got[0, 0].astype(jnp.float32) + x_got[1, 0].astype(jnp.float32)).astype(jnp.bfloat16)
        low = jnp.where(i == 0, x_got[0, 0].astype(jnp.float32), x_got[1, 0].astype(jnp.float32))
        high = jnp.where(i == 0, x_got[1, 1].astype(jnp.float32), x_got[0, 1].astype(jnp.float32))
        edge_msg[...] = (low + high).astype(jnp.bfloat16)
        for d in range(1, outer):
            launch(o + d < outer,
                   lambda d=d: copy(pair_msg, pair_got.at[d], p_sem.at[HALO + 1 + d], at(o_=o + d)))
        launch(o + 1 < outer, lambda: copy(edge_msg, edge_got, p_sem.at[HALO + 1], at(o_=o + 1)))

    def prefix():
        for d in range(1, outer):
            when(o >= d, lambda d=d: copy(pair_msg, pair_got.at[d], p_sem.at[HALO + 1 + d],
                                          at(c_=1 - c)).wait_recv())
        when(o >= 1, lambda: copy(edge_msg, edge_got, p_sem.at[HALO + 1], at(c_=1 - c)).wait_recv())
        zero = jnp.zeros(pair_msg.shape, jnp.float32)
        far = zero
        for d in range(2, outer):
            far = far + jnp.where(o >= d, pair_got[d].astype(jnp.float32), zero)
        near = jnp.where(o >= 1, pair_got[1].astype(jnp.float32), zero)
        edge = jnp.where(o >= 1, edge_got[...].astype(jnp.float32), zero)
        base = far + near
        before = jnp.where(i == 0, base, base + x_got[1, 0].astype(jnp.float32))
        second = jnp.where(i == 0, far + edge, base + x_got[1, 1].astype(jnp.float32))
        pre[0] = second.astype(jnp.bfloat16)
        pre[1] = before.astype(jnp.bfloat16)
        for d in range(1, lanes_y):
            launch(True, lambda d=d: copy(pre, pre_out.at[c, y], kv_sem.at[3 + 2 * lanes_y + d],
                                          at(y_=y_far(d))))
        locals_.append(pltpu.make_async_copy(pre, pre_out.at[c, y], own_sem.at[2]))
        locals_[2].start()

    def hand_on(out, first, own, sems):
        for d in range(1, lanes_y):
            ref = out.at[c, y_from(d)]
            copy(ref, ref, kv_sem.at[first + d], at(y_=y_far(d))).wait_recv()
        own.wait()
        launch(True, lambda: copy(out.at[c], out.at[c], sems, at(c_=1 - c)))

    for t in range(2, outer):
        z_wait(t)
        if t + 1 < outer:
            z_send(t + 1)
        for key in (2 * t - 1, 2 * t):
            x_send(key)
            sib_z(key)
        if t == 2:
            pair()
            halo(1)
        for key in (2 * t - 3, 2 * t - 2):
            x_pass(key)
        for key in ((0,) if t == 2 else (2 * t - 5, 2 * t - 4)):
            y_pass(key)
    if outer <= 2:
        pair()
        halo(1)
        y_pass(0)
    prefix()
    if outer > 2:
        for key in (2 * outer - 5, 2 * outer - 4):
            y_pass(key)
    hand_on(cum_out, 3 + lanes_y, locals_[1], kv_sem.at[1])
    for key in (2 * outer - 3, 2 * outer - 2):
        x_pass(key)
    hand_on(pre_out, 3 + 2 * lanes_y, locals_[2], kv_sem.at[2])
    for key in (2 * outer - 3, 2 * outer - 2):
        y_pass(key)

    for out, sems in ((cum_out, kv_sem.at[1]), (pre_out, kv_sem.at[2])):
        other = out.at[1 - c]
        copy(other, other, sems, at(c_=1 - c)).wait_recv()
    for f in range(HALO):
        ref = q_out.at[f]
        when(frame > 0, lambda f=f, ref=ref: copy(ref, ref, p_sem.at[f], at(c_=1 - c)).wait_recv())
    for key in keys:
        sib_wait(key)
    locals_[0].wait()
    sib_copy.wait_send()
    for cond, make in sent:
        when(cond, lambda make=make: make().wait_send())


def exchanged(keys, values, weight, queries, tall, outer, lanes_y):
    frames = keys.shape[0]
    count = 2 * outer - 1
    tile = (tall, LANES)
    half = jnp.bfloat16
    dma = pltpu.SemaphoreType.DMA
    whole = pl.BlockSpec(memory_space=pltpu.VMEM)
    anywhere = pl.BlockSpec(memory_space=pl.ANY)
    return pl.pallas_call(
        functools.partial(exchange, outer, lanes_y),
        out_shape=(
            jax.ShapeDtypeStruct((2, lanes_y, frames) + tile, half),
            jax.ShapeDtypeStruct((2, lanes_y, HALO) + tile, half),
            jax.ShapeDtypeStruct((2, 2 * outer) + weight.shape[1:], half),
            jax.ShapeDtypeStruct((HALO,) + queries.shape[1:], half),
        ),
        in_specs=[whole, whole, anywhere, anywhere],
        out_specs=(anywhere,) * 4,
        scratch_shapes=[
            pltpu.VMEM((2, lanes_y, frames) + tile, half),
            pltpu.VMEM((lanes_y, frames) + tile, half),
            pltpu.VMEM((lanes_y, frames) + tile, half),
            pltpu.VMEM((lanes_y, frames) + tile, half),
            pltpu.VMEM((frames,) + tile, jnp.float32),
            pltpu.VMEM((frames,) + tile, half),
            pltpu.VMEM((HALO,) + tile, half),
            pltpu.VMEM((2, HALO) + tile, half),
            pltpu.VMEM(tile, half),
            pltpu.VMEM(tile, half),
            pltpu.VMEM((outer,) + tile, half),
            pltpu.VMEM(tile, half),
            dma((3,)),
            dma((3 + 3 * lanes_y, 2)),
            dma((2, outer, 2)),
            dma((count, 2)),
            dma((count, lanes_y, 2)),
            dma((count, 2)),
            dma((count, 2)),
            dma((count, lanes_y, 2)),
            dma((HALO + 1 + outer, 2)),
        ],
        compiler_params=pltpu.CompilerParams(
            collective_id=0, has_side_effects=True, vmem_limit_bytes=40 * 2**20),
    )(keys, values, weight, queries)


def project(deep, q_hbm, early_hbm, cum_hbm, pre_hbm, w_hbm, taps_ref, out_ref,
            q_ref, early_ref, cum_ref, pre_ref, w_ref, head_ref, att_ref, sems):
    frames, width, tokens = q_ref.shape
    lanes_y, rows = cum_ref.shape[1], cum_ref.shape[3]
    sections, deep_pad, half = w_hbm.shape[1:]
    moves = [(q_hbm, q_ref), (early_hbm, early_ref), (pre_hbm, pre_ref), (cum_hbm, cum_ref),
             (w_hbm.at[0], w_ref.at[0]), (w_hbm.at[1], w_ref.at[1])]
    loads = [pltpu.make_async_copy(src, dst, sems.at[n]) for n, (src, dst) in enumerate(moves)]
    for load in loads:
        load.start()
    gap = jnp.zeros((LANES - HEAD_DIM, tokens), jnp.bfloat16)
    head_ref[...] = jnp.zeros(head_ref.shape, jnp.bfloat16)

    def place(channel):
        section, at = channel // deep, channel % deep
        return section * deep_pad + section * deep % 16 + at

    def state(ref, f, h):
        pieces = [ref[(p // rows) // lanes_y, (p // rows) % lanes_y, f, p % rows:p % rows + e - p]
                  for p, e in cuts(h * LANES, (h + 1) * LANES, rows)]
        return pieces[0] if len(pieces) == 1 else jnp.concatenate(pieces, axis=0)

    def attend(f, query, states):
        for h in range(HEADS):
            low, high = h * HEAD_DIM, (h + 1) * HEAD_DIM
            rows_in = jnp.maximum(query(low, high), 0)
            terms = states(h)
            sums = jnp.dot(jnp.concatenate(terms, axis=1),
                           jnp.concatenate([rows_in, gap] * len(terms), axis=0),
                           preferred_element_type=jnp.float32)
            result = sums[:HEAD_DIM] * (1.0 / (sums[HEAD_DIM:HEAD_DIM + 1] + stab_eps))
            pieces, end = [], None
            for p, e in cuts(low, high, deep):
                if end is not None:
                    pieces.append(jnp.zeros((place(p) - end, tokens), jnp.float32))
                pieces.append(result[p - low:e - low])
                end = place(e - 1) + 1
            result = pieces[0] if len(pieces) == 1 else jnp.concatenate(pieces, axis=0)
            head_ref[place(low):end] = result.astype(jnp.bfloat16)
        span = pl.ds(pl.multiple_of(f * tokens, LANES), tokens)
        att_ref[span] = head_ref[...].T

    first = lax.axis_index("frame") == 0
    for load in loads[:3]:
        load.wait()

    @pl.when(first)
    def _():
        att_ref[0:HALO * tokens] = jnp.zeros((HALO * tokens, att_ref.shape[1]), jnp.bfloat16)

    @pl.when(jnp.logical_not(first))
    def _():
        @pl.loop(0, HALO)
        def _(f):
            attend(f, lambda low, high: early_ref[f, low:high], lambda h: [state(pre_ref, f, h)])

    loads[3].wait()

    @pl.loop(0, frames)
    def _(f):
        attend(f + HALO, lambda low, high: q_ref[f, low:high],
               lambda h: [state(pre_ref, 1, h), state(cum_ref, f, h)])

    def columns(weight, start, count):
        result = jnp.dot(att_ref[...], weight, preferred_element_type=jnp.float32)
        result = result.astype(jnp.bfloat16).astype(jnp.float32)
        result = result.reshape(HALO + frames, tokens, weight.shape[1])[:, :, :count]
        span = pl.ds(start, count)
        taps = [taps_ref[n:n + 1, span] for n in range(3)]
        for f in range(frames):
            mixed = taps[0] * result[f + 2] + taps[1] * result[f + 1] + taps[2] * result[f]
            out_ref[f, span] = mixed.T.astype(jnp.bfloat16)

    deepest = sections * deep_pad
    step = 2 * LANES
    whole = half // step
    rest = half - whole * step

    def weight(n, span):
        return w_ref[n, :, :, span].reshape(deepest, span.size)

    loads[4].wait()

    @pl.loop(0, whole)
    def _(t):
        at = pl.multiple_of(t * step, step)
        columns(weight(0, pl.ds(at, step)), at, step)

    loads[5].wait()
    if rest:
        both = jnp.concatenate([weight(0, pl.ds(half - rest, rest)), weight(1, pl.ds(0, rest))], axis=1)
        columns(both, half - rest, 2 * rest)

    @pl.loop(0, whole - 1)
    def _(t):
        at = pl.multiple_of(t * step + rest, LANES)
        columns(weight(1, pl.ds(at, step)), pl.multiple_of(half + at, LANES), step)

    at = (whole - 1) * step + rest
    columns(weight(1, pl.ds(at, step)), half + at, width - half - at)


def projection(queries, earlier, cum, pre, weight, taps, deep):
    frames, width, tokens = queries.shape
    rows = (HALO + frames) * tokens
    depth = weight.shape[1] * weight.shape[2]
    whole = pl.BlockSpec(memory_space=pltpu.VMEM)
    anywhere = pl.BlockSpec(memory_space=pl.ANY)
    return pl.pallas_call(
        functools.partial(project, deep),
        out_shape=jax.ShapeDtypeStruct(queries.shape, queries.dtype),
        in_specs=[anywhere] * 5 + [whole],
        out_specs=whole,
        scratch_shapes=[pltpu.VMEM(ref.shape, ref.dtype) for ref in (queries, earlier, cum, pre, weight)] + [
            pltpu.VMEM((depth, tokens), jnp.bfloat16),
            pltpu.VMEM((rows, depth), jnp.bfloat16),
            pltpu.SemaphoreType.DMA((6,)),
        ],
        cost_estimate=pl.CostEstimate(
            flops=2 * rows * depth * width, bytes_accessed=2 * depth * width, transcendentals=0),
        compiler_params=pltpu.CompilerParams(vmem_limit_bytes=50 * 2**20),
    )(queries, earlier, cum, pre, weight, taps)


def up_to(value, multiple):
    return -(-value // multiple) * multiple


def per_device(sections, lanes, queries, keys, values, out_weight, conv_taps):
    width = queries.shape[2]
    lanes_y, outer = lanes // 2, sections // 2
    queries, keys, values = (jnp.swapaxes(a, 1, 2) for a in (queries, keys, values))
    tall = up_to(HEADS * LANES, 16 * lanes) // lanes
    deep = out_weight.shape[0]
    shift = max(n * deep % 16 for n in range(sections))
    deep_pad = up_to(deep + shift, 16 * lanes_y)
    wide = up_to(width, 2 * LANES)
    weight = lax.dynamic_update_slice(
        jnp.zeros((deep_pad, wide), out_weight.dtype), out_weight,
        (lax.rem(lax.axis_index("frame") * deep, 16), 0))
    weight = weight.reshape(deep_pad, 2, wide // 2).transpose(1, 0, 2)
    cum, pre, weight, earlier = exchanged(keys, values, weight, queries, tall, outer, lanes_y)
    mixed = projection(queries, earlier, cum, pre, weight, conv_taps, deep)
    return jnp.swapaxes(mixed, 1, 2)


def solution(mesh):
    split = P("frame", "space", None)
    return jax.shard_map(
        functools.partial(per_device, mesh.shape["frame"], mesh.shape["space"]), mesh=mesh,
        in_specs=(split, split, split, P("frame", None), P()), out_specs=split, check_vma=False)
```

```python
import functools

import jax
import jax.numpy as jnp
from jax import lax
from jax.experimental import pallas as pl
from jax.experimental.pallas import tpu as pltpu
from jax.sharding import PartitionSpec as P

HEADS = 20
HEAD_DIM = 112
LANES = 128
HALO = 2
stab_eps = 1e-06
MESH = pl.DeviceIdType.MESH


def cuts(start, stop, size):
    while start < stop:
        end = min(stop, (start // size + 1) * size)
        yield start, end
        start = end


def exchange(outer, lanes_y, k_hbm, v_hbm, w_hbm, q_in, cum_out, pre_out, w_out, q_out,
             k_in, v_in, w_own, w_in, kv_in, sib_kv, chip_kv, y_kv, frame_kv, cum, pre, x_got, pair_msg, edge_msg, pair_got, edge_got,
             own_sem, kv_sem, z_sem, x_sem, y_sem, sz_sem, sx_sem, sy_sem, p_sem):
    frame = lax.axis_index("frame")
    space = lax.axis_index("space")
    o, i = frame // 2, frame % 2
    y, c = space // 2, space % 2
    frames, tall = kv_in.shape[2], kv_in.shape[3]
    rows = w_in.shape[1]
    part = rows // lanes_y

    def at(o_=None, i_=None, y_=None, c_=None):
        o_ = o if o_ is None else o_
        i_ = i if i_ is None else i_
        y_ = y if y_ is None else y_
        c_ = c if c_ is None else c_
        return (o_ * 2 + i_, y_ * 2 + c_)

    def copy(src, dst, sems, to):
        return pltpu.make_async_remote_copy(
            src_ref=src, dst_ref=dst, send_sem=sems.at[0], recv_sem=sems.at[1],
            device_id=to, device_id_type=MESH)

    def when(cond, do):
        if cond is True:
            do()
        else:
            pl.when(cond)(do)

    def y_far(d):
        return lax.rem(y + d, lanes_y)

    def y_from(d):
        return lax.rem(y + lanes_y - d, lanes_y)

    incoming = [pltpu.make_async_copy(src, dst, own_sem.at[3 + n])
                for n, (src, dst) in enumerate(((w_hbm, w_own), (k_hbm, k_in), (v_hbm, v_in)))]
    for load in incoming:
        load.start()

    barrier = pltpu.get_barrier_semaphore()

    def greet(to):
        pl.semaphore_signal(barrier, inc=1, device_id=to, device_id_type=MESH)

    for d in range(1, outer):
        greet(at(o_=lax.rem(o + d, outer)))
    for d in range(1, lanes_y):
        greet(at(y_=y_far(d)))
    greet(at(i_=1 - i))
    greet(at(c_=1 - c))
    into = jnp.logical_and(i == 0, o > 0)
    onto = jnp.logical_and(i == 1, o < outer - 1)
    when(into, lambda: greet(at(o_=o - 1, i_=1)))
    when(onto, lambda: greet(at(o_=o + 1, i_=0)))
    deep, width = w_own.shape
    half = w_in.shape[2]
    w_in[...] = jnp.zeros(w_in.shape, jnp.bfloat16)
    incoming[0].wait()
    for shift in sorted({n * deep % 16 for n in range(2 * outer)}):
        def lay(shift=shift):
            w_in[0, shift:shift + deep, :] = w_own[:, :half]
            w_in[1, shift:shift + deep, :width - half] = w_own[:, half:]
        pl.when(lax.rem(frame * deep, 16) == shift)(lay)

    peers = (outer - 1) + (lanes_y - 1) + 2
    pl.semaphore_wait(barrier, peers + jnp.where(jnp.logical_or(into, onto), 1, 0))

    def source(key):
        t = (key + 1) // 2
        if key == 0:
            return o, True
        if key % 2:
            return o - t, o >= t
        return o + t, o + t < outer

    keys = range(2 * outer - 1)
    sent = []

    def launch(cond, make):
        when(cond, lambda: make().start())
        sent.append((cond, make))

    def mine(key):
        return w_out.at[c, source(key)[0] * 2 + i]

    def theirs(key, y_):
        span = pl.ds(pl.multiple_of(y_ * part, 16), part)
        return w_out.at[c, source(key)[0] * 2 + 1 - i, span]

    def z_copy(up, t):
        g = ((o - t + 1) if up else (o + t - 1)) * 2 + i
        dst = w_out.at[c, g]
        return copy(w_in.at[c] if t == 1 else dst, dst, z_sem.at[0 if up else 1, t],
                    at(o_=o + 1 if up else o - 1))

    def z_send(t):
        launch(jnp.logical_and(o < outer - 1, o - t + 1 >= 0), lambda: z_copy(True, t))
        launch(jnp.logical_and(o > 0, o + t - 1 < outer), lambda: z_copy(False, t))

    def z_wait(t):
        def got(key, up):
            ref = mine(key)
            copy(ref, ref, z_sem.at[0 if up else 1, t], at(c_=1 - c)).wait_recv()
        when(source(2 * t - 1)[1], lambda: got(2 * t - 1, True))
        when(source(2 * t)[1], lambda: got(2 * t, False))

    def x_copy(key):
        span = pl.ds(pl.multiple_of(y * part, 16), part)
        src = w_in.at[c, span] if key == 0 else mine(key).at[span]
        return copy(src, mine(key).at[span], x_sem.at[key], at(i_=1 - i))

    def x_send(key):
        launch(source(key)[1], lambda: x_copy(key))

    def sib_z(key):
        launch(source(key)[1], lambda: copy(mine(key), mine(key), sz_sem.at[key], at(c_=1 - c)))

    def x_pass(key):
        def got():
            ref = theirs(key, y)
            copy(ref, ref, x_sem.at[key], at(i_=1 - i)).wait_recv()
        cond = source(key)[1]
        when(cond, got)
        for d in range(1, lanes_y):
            launch(cond, lambda d=d: copy(theirs(key, y), theirs(key, y), y_sem.at[key, d],
                                          at(y_=y_far(d))))
        launch(cond, lambda: copy(theirs(key, y), theirs(key, y), sx_sem.at[key], at(c_=1 - c)))

    def y_pass(key):
        cond = source(key)[1]
        for d in range(1, lanes_y):
            def got(d=d):
                ref = theirs(key, y_from(d))
                copy(ref, ref, y_sem.at[key, d], at(y_=y_far(d))).wait_recv()
            when(cond, got)
            launch(cond, lambda d=d: copy(theirs(key, y_from(d)), theirs(key, y_from(d)),
                                          sy_sem.at[key, d], at(c_=1 - c)))

    def sib_wait(key):
        cond = source(key)[1]
        g = source(key)[0] * 2

        def got(ref, sems):
            copy(ref, ref, sems, at(c_=1 - c)).wait_recv()
        if key:
            when(cond, lambda: got(w_out.at[1 - c, g + i], sz_sem.at[key]))
        for d in range(lanes_y):
            span = pl.ds(pl.multiple_of(y_from(d) * part, 16), part)
            sems = sx_sem.at[key] if d == 0 else sy_sem.at[key, d]
            when(cond, lambda span=span, sems=sems: got(w_out.at[1 - c, g + 1 - i, span], sems))

    z_send(1)
    x_send(0)
    locals_ = [pltpu.make_async_copy(w_in, w_out.at[:, frame], own_sem.at[0])]
    locals_[0].start()

    def halo(f):
        launch(frame < 2 * outer - 1,
               lambda: copy(q_in.at[frames - HALO + f], q_out.at[f], p_sem.at[f], (frame + 1, space)))

    for load in incoming[1:]:
        load.wait()

    tokens = k_in.shape[2]
    gap = LANES - HEAD_DIM
    nothing = jnp.zeros((gap, tokens), jnp.bfloat16)
    ones = jnp.ones((gap, tokens), jnp.bfloat16)

    @pl.loop(0, frames)
    def _(f):
        for h in range(HEADS):
            span = slice(h * HEAD_DIM, (h + 1) * HEAD_DIM)
            key = jnp.concatenate([jnp.maximum(k_in[f, span], 0), nothing], axis=0)
            value = jnp.concatenate([v_in[f, span], ones], axis=0)
            sums = lax.dot_general(value, key, (((1,), (1,)), ((), ())),
                                   preferred_element_type=jnp.float32).astype(jnp.bfloat16)
            for p, e in cuts(h * LANES, (h + 1) * LANES, tall):
                n = p // tall
                kv_in[n // lanes_y, n % lanes_y, f, p % tall:p % tall + e - p] = (
                    sums[p - h * LANES:e - h * LANES])

    sib_copy = copy(kv_in.at[1 - c], sib_kv, kv_sem.at[0], at(c_=1 - c))
    sib_copy.start()
    sib_copy.wait_recv()
    for d in list(range(1, lanes_y)) + [0]:
        to = y_far(d)
        for f in range(frames):
            chip_kv[to, f] = (kv_in[c, to, f].astype(jnp.float32)
                              + sib_kv[to, f].astype(jnp.float32)).astype(jnp.bfloat16)
        if d:
            launch(True, lambda d=d: copy(chip_kv.at[y_far(d)], y_kv.at[d], kv_sem.at[3 + d],
                                          at(y_=y_far(d))))
    halo(0)
    z_wait(1)
    if outer > 2:
        z_send(2)
    for key in (1, 2):
        x_send(key)
        sib_z(key)
    for d in range(1, lanes_y):
        copy(chip_kv.at[y_far(d)], y_kv.at[d], kv_sem.at[3 + d], at(y_=y_far(d))).wait_recv()
    for f in range(frames):
        total = chip_kv[y, f].astype(jnp.float32)
        for d in range(1, lanes_y):
            total = total + y_kv[d, f].astype(jnp.float32)
        frame_kv[f] = total if f == 0 else frame_kv[f - 1] + total
    for f in range(HALO):
        x_got[0, f] = frame_kv[frames - 1 - f].astype(jnp.bfloat16)
    launch(True, lambda: copy(x_got.at[0], x_got.at[1], p_sem.at[HALO], at(i_=1 - i)))
    for f in range(frames):
        cum[f] = frame_kv[f].astype(jnp.bfloat16)
    for d in range(1, lanes_y):
        launch(True, lambda d=d: copy(cum, cum_out.at[c, y], kv_sem.at[3 + lanes_y + d], at(y_=y_far(d))))
    locals_.append(pltpu.make_async_copy(cum, cum_out.at[c, y], own_sem.at[1]))
    locals_[1].start()
    x_pass(0)

    def pair():
        copy(x_got.at[0], x_got.at[1], p_sem.at[HALO], at(i_=1 - i)).wait_recv()
        pair_msg[...] = (x_got[0, 0].astype(jnp.float32) + x_got[1, 0].astype(jnp.float32)).astype(jnp.bfloat16)
        low = jnp.where(i == 0, x_got[0, 0].astype(jnp.float32), x_got[1, 0].astype(jnp.float32))
        high = jnp.where(i == 0, x_got[1, 1].astype(jnp.float32), x_got[0, 1].astype(jnp.float32))
        edge_msg[...] = (low + high).astype(jnp.bfloat16)
        for d in range(1, outer):
            launch(o + d < outer,
                   lambda d=d: copy(pair_msg, pair_got.at[d], p_sem.at[HALO + 1 + d], at(o_=o + d)))
        launch(o + 1 < outer, lambda: copy(edge_msg, edge_got, p_sem.at[HALO + 1], at(o_=o + 1)))

    def prefix():
        for d in range(1, outer):
            when(o >= d, lambda d=d: copy(pair_msg, pair_got.at[d], p_sem.at[HALO + 1 + d],
                                          at(c_=1 - c)).wait_recv())
        when(o >= 1, lambda: copy(edge_msg, edge_got, p_sem.at[HALO + 1], at(c_=1 - c)).wait_recv())
        zero = jnp.zeros(pair_msg.shape, jnp.float32)
        far = zero
        for d in range(2, outer):
            far = far + jnp.where(o >= d, pair_got[d].astype(jnp.float32), zero)
        near = jnp.where(o >= 1, pair_got[1].astype(jnp.float32), zero)
        edge = jnp.where(o >= 1, edge_got[...].astype(jnp.float32), zero)
        base = far + near
        before = jnp.where(i == 0, base, base + x_got[1, 0].astype(jnp.float32))
        second = jnp.where(i == 0, far + edge, base + x_got[1, 1].astype(jnp.float32))
        pre[0] = second.astype(jnp.bfloat16)
        pre[1] = before.astype(jnp.bfloat16)
        for d in range(1, lanes_y):
            launch(True, lambda d=d: copy(pre, pre_out.at[c, y], kv_sem.at[3 + 2 * lanes_y + d],
                                          at(y_=y_far(d))))
        locals_.append(pltpu.make_async_copy(pre, pre_out.at[c, y], own_sem.at[2]))
        locals_[2].start()

    def hand_on(out, first, own, sems):
        for d in range(1, lanes_y):
            ref = out.at[c, y_from(d)]
            copy(ref, ref, kv_sem.at[first + d], at(y_=y_far(d))).wait_recv()
        own.wait()
        launch(True, lambda: copy(out.at[c], out.at[c], sems, at(c_=1 - c)))

    for t in range(2, outer):
        z_wait(t)
        if t + 1 < outer:
            z_send(t + 1)
        for key in (2 * t - 1, 2 * t):
            x_send(key)
            sib_z(key)
        if t == 2:
            pair()
            halo(1)
        for key in (2 * t - 3, 2 * t - 2):
            x_pass(key)
        for key in ((0,) if t == 2 else (2 * t - 5, 2 * t - 4)):
            y_pass(key)
    if outer <= 2:
        pair()
        halo(1)
        y_pass(0)
    prefix()
    if outer > 2:
        for key in (2 * outer - 5, 2 * outer - 4):
            y_pass(key)
    hand_on(cum_out, 3 + lanes_y, locals_[1], kv_sem.at[1])
    for key in (2 * outer - 3, 2 * outer - 2):
        x_pass(key)
    hand_on(pre_out, 3 + 2 * lanes_y, locals_[2], kv_sem.at[2])
    for key in (2 * outer - 3, 2 * outer - 2):
        y_pass(key)

    for out, sems in ((cum_out, kv_sem.at[1]), (pre_out, kv_sem.at[2])):
        other = out.at[1 - c]
        copy(other, other, sems, at(c_=1 - c)).wait_recv()
    for f in range(HALO):
        ref = q_out.at[f]
        when(frame > 0, lambda f=f, ref=ref: copy(ref, ref, p_sem.at[f], at(c_=1 - c)).wait_recv())
    for key in keys:
        sib_wait(key)
    locals_[0].wait()
    sib_copy.wait_send()
    for cond, make in sent:
        when(cond, lambda make=make: make().wait_send())


def exchanged(keys, values, weight, queries, padded, tall, outer, lanes_y):
    frames = keys.shape[0]
    count = 2 * outer - 1
    tile = (tall, LANES)
    half = jnp.bfloat16
    dma = pltpu.SemaphoreType.DMA
    anywhere = pl.BlockSpec(memory_space=pl.ANY)
    return pl.pallas_call(
        functools.partial(exchange, outer, lanes_y),
        out_shape=(
            jax.ShapeDtypeStruct((2, lanes_y, frames) + tile, half),
            jax.ShapeDtypeStruct((2, lanes_y, HALO) + tile, half),
            jax.ShapeDtypeStruct((2, 2 * outer) + padded, half),
            jax.ShapeDtypeStruct((HALO,) + queries.shape[1:], half),
        ),
        in_specs=[anywhere] * 4,
        out_specs=(anywhere,) * 4,
        scratch_shapes=[
            pltpu.VMEM(keys.shape, half),
            pltpu.VMEM(values.shape, half),
            pltpu.VMEM(weight.shape, half),
            pltpu.VMEM((2,) + padded, half),
            pltpu.VMEM((2, lanes_y, frames) + tile, half),
            pltpu.VMEM((lanes_y, frames) + tile, half),
            pltpu.VMEM((lanes_y, frames) + tile, half),
            pltpu.VMEM((lanes_y, frames) + tile, half),
            pltpu.VMEM((frames,) + tile, jnp.float32),
            pltpu.VMEM((frames,) + tile, half),
            pltpu.VMEM((HALO,) + tile, half),
            pltpu.VMEM((2, HALO) + tile, half),
            pltpu.VMEM(tile, half),
            pltpu.VMEM(tile, half),
            pltpu.VMEM((outer,) + tile, half),
            pltpu.VMEM(tile, half),
            dma((6,)),
            dma((3 + 3 * lanes_y, 2)),
            dma((2, outer, 2)),
            dma((count, 2)),
            dma((count, lanes_y, 2)),
            dma((count, 2)),
            dma((count, 2)),
            dma((count, lanes_y, 2)),
            dma((HALO + 1 + outer, 2)),
        ],
        compiler_params=pltpu.CompilerParams(
            collective_id=0, has_side_effects=True, vmem_limit_bytes=56 * 2**20),
    )(keys, values, weight, queries)


def project(deep, q_hbm, early_hbm, cum_hbm, pre_hbm, w_hbm, taps_ref, out_ref,
            q_ref, early_ref, cum_ref, pre_ref, w_ref, head_ref, att_ref, sems):
    frames, width, tokens = q_ref.shape
    lanes_y, rows = cum_ref.shape[1], cum_ref.shape[3]
    sections, deep_pad, half = w_hbm.shape[1:]
    moves = [(q_hbm, q_ref), (early_hbm, early_ref), (pre_hbm, pre_ref), (cum_hbm, cum_ref),
             (w_hbm.at[0], w_ref.at[0]), (w_hbm.at[1], w_ref.at[1])]
    loads = [pltpu.make_async_copy(src, dst, sems.at[n]) for n, (src, dst) in enumerate(moves)]
    for load in loads:
        load.start()
    gap = jnp.zeros((LANES - HEAD_DIM, tokens), jnp.bfloat16)
    head_ref[...] = jnp.zeros(head_ref.shape, jnp.bfloat16)

    def place(channel):
        section, at = channel // deep, channel % deep
        return section * deep_pad + section * deep % 16 + at

    def state(ref, f, h):
        pieces = [ref[(p // rows) // lanes_y, (p // rows) % lanes_y, f, p % rows:p % rows + e - p]
                  for p, e in cuts(h * LANES, (h + 1) * LANES, rows)]
        return pieces[0] if len(pieces) == 1 else jnp.concatenate(pieces, axis=0)

    def attend(f, query, states):
        for h in range(HEADS):
            low, high = h * HEAD_DIM, (h + 1) * HEAD_DIM
            rows_in = jnp.maximum(query(low, high), 0)
            terms = states(h)
            sums = jnp.dot(jnp.concatenate(terms, axis=1),
                           jnp.concatenate([rows_in, gap] * len(terms), axis=0),
                           preferred_element_type=jnp.float32)
            result = sums[:HEAD_DIM] * (1.0 / (sums[HEAD_DIM:HEAD_DIM + 1] + stab_eps))
            pieces, end = [], None
            for p, e in cuts(low, high, deep):
                if end is not None:
                    pieces.append(jnp.zeros((place(p) - end, tokens), jnp.float32))
                pieces.append(result[p - low:e - low])
                end = place(e - 1) + 1
            result = pieces[0] if len(pieces) == 1 else jnp.concatenate(pieces, axis=0)
            head_ref[place(low):end] = result.astype(jnp.bfloat16)
        span = pl.ds(pl.multiple_of(f * tokens, LANES), tokens)
        att_ref[span] = head_ref[...].T

    first = lax.axis_index("frame") == 0
    for load in loads[:3]:
        load.wait()

    @pl.when(first)
    def _():
        att_ref[0:HALO * tokens] = jnp.zeros((HALO * tokens, att_ref.shape[1]), jnp.bfloat16)

    @pl.when(jnp.logical_not(first))
    def _():
        @pl.loop(0, HALO)
        def _(f):
            attend(f, lambda low, high: early_ref[f, low:high], lambda h: [state(pre_ref, f, h)])

    loads[3].wait()

    @pl.loop(0, frames)
    def _(f):
        attend(f + HALO, lambda low, high: q_ref[f, low:high],
               lambda h: [state(pre_ref, 1, h), state(cum_ref, f, h)])

    def columns(weight, start, count):
        result = jnp.dot(att_ref[...], weight, preferred_element_type=jnp.float32)
        result = result.astype(jnp.bfloat16).astype(jnp.float32)
        result = result.reshape(HALO + frames, tokens, weight.shape[1])[:, :, :count]
        span = pl.ds(start, count)
        taps = [taps_ref[n:n + 1, span] for n in range(3)]
        for f in range(frames):
            mixed = taps[0] * result[f + 2] + taps[1] * result[f + 1] + taps[2] * result[f]
            out_ref[f, span] = mixed.T.astype(jnp.bfloat16)

    deepest = sections * deep_pad
    step = 2 * LANES
    whole = half // step
    rest = half - whole * step

    def weight(n, span):
        return w_ref[n, :, :, span].reshape(deepest, span.size)

    loads[4].wait()

    @pl.loop(0, whole)
    def _(t):
        at = pl.multiple_of(t * step, step)
        columns(weight(0, pl.ds(at, step)), at, step)

    loads[5].wait()
    if rest:
        both = jnp.concatenate([weight(0, pl.ds(half - rest, rest)), weight(1, pl.ds(0, rest))], axis=1)
        columns(both, half - rest, 2 * rest)

    @pl.loop(0, whole - 1)
    def _(t):
        at = pl.multiple_of(t * step + rest, LANES)
        columns(weight(1, pl.ds(at, step)), pl.multiple_of(half + at, LANES), step)

    at = (whole - 1) * step + rest
    columns(weight(1, pl.ds(at, step)), half + at, width - half - at)


def projection(queries, earlier, cum, pre, weight, taps, deep):
    frames, width, tokens = queries.shape
    rows = (HALO + frames) * tokens
    depth = weight.shape[1] * weight.shape[2]
    whole = pl.BlockSpec(memory_space=pltpu.VMEM)
    anywhere = pl.BlockSpec(memory_space=pl.ANY)
    return pl.pallas_call(
        functools.partial(project, deep),
        out_shape=jax.ShapeDtypeStruct(queries.shape, queries.dtype),
        in_specs=[anywhere] * 5 + [whole],
        out_specs=whole,
        scratch_shapes=[pltpu.VMEM(ref.shape, ref.dtype) for ref in (queries, earlier, cum, pre, weight)] + [
            pltpu.VMEM((depth, tokens), jnp.bfloat16),
            pltpu.VMEM((rows, depth), jnp.bfloat16),
            pltpu.SemaphoreType.DMA((6,)),
        ],
        cost_estimate=pl.CostEstimate(
            flops=2 * rows * depth * width, bytes_accessed=2 * depth * width, transcendentals=0),
        compiler_params=pltpu.CompilerParams(vmem_limit_bytes=58 * 2**20),
    )(queries, earlier, cum, pre, weight, taps)


def up_to(value, multiple):
    return -(-value // multiple) * multiple


def per_device(sections, lanes, queries, keys, values, out_weight, conv_taps):
    width = queries.shape[2]
    lanes_y, outer = lanes // 2, sections // 2
    queries, keys, values = (jnp.swapaxes(a, 1, 2) for a in (queries, keys, values))
    tall = up_to(HEADS * LANES, 16 * lanes) // lanes
    deep = out_weight.shape[0]
    shift = max(n * deep % 16 for n in range(sections))
    padded = (up_to(deep + shift, 16 * lanes_y), up_to(width, 2 * LANES) // 2)
    cum, pre, weight, earlier = exchanged(
        keys, values, out_weight, queries, padded, tall, outer, lanes_y)
    mixed = projection(queries, earlier, cum, pre, weight, conv_taps, deep)
    return jnp.swapaxes(mixed, 1, 2)


def solution(mesh):
    split = P("frame", "space", None)
    return jax.shard_map(
        functools.partial(per_device, mesh.shape["frame"], mesh.shape["space"]), mesh=mesh,
        in_specs=(split, split, split, P("frame", None), P()), out_specs=split, check_vma=False)
```

```python
import functools

import jax
import jax.numpy as jnp
from jax import lax
from jax.experimental import pallas as pl
from jax.experimental.pallas import tpu as pltpu
from jax.sharding import PartitionSpec as P

HEADS = 20
HEAD_DIM = 112
LANES = 128
HALO = 2
stab_eps = 1e-06
MESH = pl.DeviceIdType.MESH


def cuts(start, stop, size):
    while start < stop:
        end = min(stop, (start // size + 1) * size)
        yield start, end
        start = end


def exchange(outer, lanes_y, k_hbm, v_hbm, w_hbm, q_in, cum_out, pre_out, w_out, q_out,
             k_in, v_in, w_own, w_in, kv_in, sib_kv, chip_kv, y_kv, frame_kv, cum, pre, x_got, pair_msg, edge_msg, pair_got, edge_got, relay,
             own_sem, kv_sem, z_sem, x_sem, y_sem, sz_sem, sx_sem, sy_sem, p_sem):
    frame = lax.axis_index("frame")
    space = lax.axis_index("space")
    o, i = frame // 2, frame % 2
    y, c = space // 2, space % 2
    frames, tall = kv_in.shape[2], kv_in.shape[3]
    rows = w_in.shape[1]
    part = rows // lanes_y

    def at(o_=None, i_=None, y_=None, c_=None):
        o_ = o if o_ is None else o_
        i_ = i if i_ is None else i_
        y_ = y if y_ is None else y_
        c_ = c if c_ is None else c_
        return (o_ * 2 + i_, y_ * 2 + c_)

    def copy(src, dst, sems, to):
        return pltpu.make_async_remote_copy(
            src_ref=src, dst_ref=dst, send_sem=sems.at[0], recv_sem=sems.at[1],
            device_id=to, device_id_type=MESH)

    def when(cond, do):
        if cond is True:
            do()
        else:
            pl.when(cond)(do)

    def y_far(d):
        return lax.rem(y + d, lanes_y)

    def y_from(d):
        return lax.rem(y + lanes_y - d, lanes_y)

    incoming = [pltpu.make_async_copy(src, dst, own_sem.at[3 + n])
                for n, (src, dst) in enumerate(((w_hbm, w_own), (k_hbm, k_in), (v_hbm, v_in)))]
    for load in incoming:
        load.start()

    barrier = pltpu.get_barrier_semaphore()

    def greet(to):
        pl.semaphore_signal(barrier, inc=1, device_id=to, device_id_type=MESH)

    for d in range(1, outer):
        greet(at(o_=lax.rem(o + d, outer)))
    for d in range(1, lanes_y):
        greet(at(y_=y_far(d)))
    greet(at(i_=1 - i))
    greet(at(c_=1 - c))
    deep, width = w_own.shape
    half = w_in.shape[2]
    w_in[...] = jnp.zeros(w_in.shape, jnp.bfloat16)
    incoming[0].wait()
    for shift in sorted({n * deep % 16 for n in range(2 * outer)}):
        def lay(shift=shift):
            w_in[0, shift:shift + deep, :] = w_own[:, :half]
            w_in[1, shift:shift + deep, :width - half] = w_own[:, half:]
        pl.when(lax.rem(frame * deep, 16) == shift)(lay)

    peers = (outer - 1) + (lanes_y - 1) + 2
    pl.semaphore_wait(barrier, peers)

    def source(key):
        t = (key + 1) // 2
        if key == 0:
            return o, True
        if key % 2:
            return o - t, o >= t
        return o + t, o + t < outer

    keys = range(2 * outer - 1)
    sent = []

    def launch(cond, make):
        when(cond, lambda: make().start())
        sent.append((cond, make))

    def mine(key):
        return w_out.at[c, source(key)[0] * 2 + i]

    def theirs(key, y_):
        span = pl.ds(pl.multiple_of(y_ * part, 16), part)
        return w_out.at[c, source(key)[0] * 2 + 1 - i, span]

    def z_copy(up, t):
        g = ((o - t + 1) if up else (o + t - 1)) * 2 + i
        dst = w_out.at[c, g]
        return copy(w_in.at[c] if t == 1 else dst, dst, z_sem.at[0 if up else 1, t],
                    at(o_=o + 1 if up else o - 1))

    def z_send(t):
        launch(jnp.logical_and(o < outer - 1, o - t + 1 >= 0), lambda: z_copy(True, t))
        launch(jnp.logical_and(o > 0, o + t - 1 < outer), lambda: z_copy(False, t))

    def z_wait(t):
        def got(key, up):
            ref = mine(key)
            copy(ref, ref, z_sem.at[0 if up else 1, t], at(c_=1 - c)).wait_recv()
        when(source(2 * t - 1)[1], lambda: got(2 * t - 1, True))
        when(source(2 * t)[1], lambda: got(2 * t, False))

    def x_copy(key):
        span = pl.ds(pl.multiple_of(y * part, 16), part)
        src = w_in.at[c, span] if key == 0 else mine(key).at[span]
        return copy(src, mine(key).at[span], x_sem.at[key], at(i_=1 - i))

    def x_send(key):
        launch(source(key)[1], lambda: x_copy(key))

    def sib_z(key):
        launch(source(key)[1], lambda: copy(mine(key), mine(key), sz_sem.at[key], at(c_=1 - c)))

    def x_pass(key):
        def got():
            ref = theirs(key, y)
            copy(ref, ref, x_sem.at[key], at(i_=1 - i)).wait_recv()
        cond = source(key)[1]
        when(cond, got)
        for d in range(1, lanes_y):
            launch(cond, lambda d=d: copy(theirs(key, y), theirs(key, y), y_sem.at[key, d],
                                          at(y_=y_far(d))))
        launch(cond, lambda: copy(theirs(key, y), theirs(key, y), sx_sem.at[key], at(c_=1 - c)))

    def y_pass(key):
        cond = source(key)[1]
        for d in range(1, lanes_y):
            def got(d=d):
                ref = theirs(key, y_from(d))
                copy(ref, ref, y_sem.at[key, d], at(y_=y_far(d))).wait_recv()
            when(cond, got)
            launch(cond, lambda d=d: copy(theirs(key, y_from(d)), theirs(key, y_from(d)),
                                          sy_sem.at[key, d], at(c_=1 - c)))

    def sib_wait(key):
        cond = source(key)[1]
        g = source(key)[0] * 2

        def got(ref, sems):
            copy(ref, ref, sems, at(c_=1 - c)).wait_recv()
        if key:
            when(cond, lambda: got(w_out.at[1 - c, g + i], sz_sem.at[key]))
        for d in range(lanes_y):
            span = pl.ds(pl.multiple_of(y_from(d) * part, 16), part)
            sems = sx_sem.at[key] if d == 0 else sy_sem.at[key, d]
            when(cond, lambda span=span, sems=sems: got(w_out.at[1 - c, g + 1 - i, span], sems))

    z_send(1)
    x_send(0)
    locals_ = [pltpu.make_async_copy(w_in, w_out.at[:, frame], own_sem.at[0])]
    locals_[0].start()

    via = HALO + 1 + outer
    onward = jnp.logical_and(i == 1, o < outer - 1)
    last = frames - HALO

    def halo_pair(f):
        launch(i == 0, lambda: copy(q_in.at[last + f], q_out.at[f], p_sem.at[f], at(i_=1)))

    def halo_onward():
        launch(onward, lambda: copy(q_in.at[last], relay, p_sem.at[via], at(i_=0)))
        launch(onward, lambda: copy(q_in.at[last + 1], relay, p_sem.at[via + 1], at(o_=o + 1)))

    def halo_pass():
        lower = jnp.logical_and(i == 0, o < outer - 1)
        upper = jnp.logical_and(i == 1, o > 0)
        when(lower, lambda: copy(relay, relay, p_sem.at[via], at(c_=1 - c)).wait_recv())
        launch(lower, lambda: copy(relay, q_out.at[0], p_sem.at[via + 2], at(o_=o + 1)))
        when(upper, lambda: copy(relay, relay, p_sem.at[via + 1], at(c_=1 - c)).wait_recv())
        launch(upper, lambda: copy(relay, q_out.at[1], p_sem.at[via + 3], at(i_=0)))

    for load in incoming[1:]:
        load.wait()

    tokens = k_in.shape[2]
    gap = LANES - HEAD_DIM
    nothing = jnp.zeros((gap, tokens), jnp.bfloat16)
    ones = jnp.ones((gap, tokens), jnp.bfloat16)

    @pl.loop(0, frames)
    def _(f):
        for h in range(HEADS):
            span = slice(h * HEAD_DIM, (h + 1) * HEAD_DIM)
            key = jnp.concatenate([jnp.maximum(k_in[f, span], 0), nothing], axis=0)
            value = jnp.concatenate([v_in[f, span], ones], axis=0)
            sums = lax.dot_general(value, key, (((1,), (1,)), ((), ())),
                                   preferred_element_type=jnp.float32).astype(jnp.bfloat16)
            for p, e in cuts(h * LANES, (h + 1) * LANES, tall):
                n = p // tall
                kv_in[n // lanes_y, n % lanes_y, f, p % tall:p % tall + e - p] = (
                    sums[p - h * LANES:e - h * LANES])

    sib_copy = copy(kv_in.at[1 - c], sib_kv, kv_sem.at[0], at(c_=1 - c))
    sib_copy.start()
    sib_copy.wait_recv()
    for d in list(range(1, lanes_y)) + [0]:
        to = y_far(d)
        for f in range(frames):
            chip_kv[to, f] = (kv_in[c, to, f].astype(jnp.float32)
                              + sib_kv[to, f].astype(jnp.float32)).astype(jnp.bfloat16)
        if d:
            launch(True, lambda d=d: copy(chip_kv.at[y_far(d)], y_kv.at[d], kv_sem.at[3 + d],
                                          at(y_=y_far(d))))
    halo_pair(0)
    halo_onward()
    z_wait(1)
    if outer > 2:
        z_send(2)
    for key in (1, 2):
        x_send(key)
        sib_z(key)
    for d in range(1, lanes_y):
        copy(chip_kv.at[y_far(d)], y_kv.at[d], kv_sem.at[3 + d], at(y_=y_far(d))).wait_recv()
    for f in range(frames):
        total = chip_kv[y, f].astype(jnp.float32)
        for d in range(1, lanes_y):
            total = total + y_kv[d, f].astype(jnp.float32)
        frame_kv[f] = total if f == 0 else frame_kv[f - 1] + total
    for f in range(HALO):
        x_got[0, f] = frame_kv[frames - 1 - f].astype(jnp.bfloat16)
    launch(True, lambda: copy(x_got.at[0], x_got.at[1], p_sem.at[HALO], at(i_=1 - i)))
    for f in range(frames):
        cum[f] = frame_kv[f].astype(jnp.bfloat16)
    for d in range(1, lanes_y):
        launch(True, lambda d=d: copy(cum, cum_out.at[c, y], kv_sem.at[3 + lanes_y + d], at(y_=y_far(d))))
    locals_.append(pltpu.make_async_copy(cum, cum_out.at[c, y], own_sem.at[1]))
    locals_[1].start()
    x_pass(0)

    def pair():
        copy(x_got.at[0], x_got.at[1], p_sem.at[HALO], at(i_=1 - i)).wait_recv()
        pair_msg[...] = (x_got[0, 0].astype(jnp.float32) + x_got[1, 0].astype(jnp.float32)).astype(jnp.bfloat16)
        low = jnp.where(i == 0, x_got[0, 0].astype(jnp.float32), x_got[1, 0].astype(jnp.float32))
        high = jnp.where(i == 0, x_got[1, 1].astype(jnp.float32), x_got[0, 1].astype(jnp.float32))
        edge_msg[...] = (low + high).astype(jnp.bfloat16)
        for d in range(1, outer):
            launch(o + d < outer,
                   lambda d=d: copy(pair_msg, pair_got.at[d], p_sem.at[HALO + 1 + d], at(o_=o + d)))
        launch(o + 1 < outer, lambda: copy(edge_msg, edge_got, p_sem.at[HALO + 1], at(o_=o + 1)))

    def prefix():
        for d in range(1, outer):
            when(o >= d, lambda d=d: copy(pair_msg, pair_got.at[d], p_sem.at[HALO + 1 + d],
                                          at(c_=1 - c)).wait_recv())
        when(o >= 1, lambda: copy(edge_msg, edge_got, p_sem.at[HALO + 1], at(c_=1 - c)).wait_recv())
        zero = jnp.zeros(pair_msg.shape, jnp.float32)
        far = zero
        for d in range(2, outer):
            far = far + jnp.where(o >= d, pair_got[d].astype(jnp.float32), zero)
        near = jnp.where(o >= 1, pair_got[1].astype(jnp.float32), zero)
        edge = jnp.where(o >= 1, edge_got[...].astype(jnp.float32), zero)
        base = far + near
        before = jnp.where(i == 0, base, base + x_got[1, 0].astype(jnp.float32))
        second = jnp.where(i == 0, far + edge, base + x_got[1, 1].astype(jnp.float32))
        pre[0] = second.astype(jnp.bfloat16)
        pre[1] = before.astype(jnp.bfloat16)
        for d in range(1, lanes_y):
            launch(True, lambda d=d: copy(pre, pre_out.at[c, y], kv_sem.at[3 + 2 * lanes_y + d],
                                          at(y_=y_far(d))))
        locals_.append(pltpu.make_async_copy(pre, pre_out.at[c, y], own_sem.at[2]))
        locals_[2].start()

    def hand_on(out, first, own, sems):
        for d in range(1, lanes_y):
            ref = out.at[c, y_from(d)]
            copy(ref, ref, kv_sem.at[first + d], at(y_=y_far(d))).wait_recv()
        own.wait()
        launch(True, lambda: copy(out.at[c], out.at[c], sems, at(c_=1 - c)))

    for t in range(2, outer):
        z_wait(t)
        if t + 1 < outer:
            z_send(t + 1)
        for key in (2 * t - 1, 2 * t):
            x_send(key)
            sib_z(key)
        if t == 2:
            pair()
            halo_pair(1)
            halo_pass()
        for key in (2 * t - 3, 2 * t - 2):
            x_pass(key)
        for key in ((0,) if t == 2 else (2 * t - 5, 2 * t - 4)):
            y_pass(key)
    if outer <= 2:
        pair()
        halo_pair(1)
        halo_pass()
        y_pass(0)
    prefix()
    if outer > 2:
        for key in (2 * outer - 5, 2 * outer - 4):
            y_pass(key)
    hand_on(cum_out, 3 + lanes_y, locals_[1], kv_sem.at[1])
    for key in (2 * outer - 3, 2 * outer - 2):
        x_pass(key)
    hand_on(pre_out, 3 + 2 * lanes_y, locals_[2], kv_sem.at[2])
    for key in (2 * outer - 3, 2 * outer - 2):
        y_pass(key)

    for out, sems in ((cum_out, kv_sem.at[1]), (pre_out, kv_sem.at[2])):
        other = out.at[1 - c]
        copy(other, other, sems, at(c_=1 - c)).wait_recv()
    for f in range(HALO):
        def landed(sems, f):
            copy(q_out.at[f], q_out.at[f], sems, at(c_=1 - c)).wait_recv()
        when(i == 1, lambda f=f: landed(p_sem.at[f], f))
        when(jnp.logical_and(i == 0, o > 0), lambda f=f: landed(p_sem.at[via + 2 + f], f))
    for key in keys:
        sib_wait(key)
    locals_[0].wait()
    sib_copy.wait_send()
    for cond, make in sent:
        when(cond, lambda make=make: make().wait_send())


def exchanged(keys, values, weight, queries, padded, tall, outer, lanes_y):
    frames = keys.shape[0]
    count = 2 * outer - 1
    tile = (tall, LANES)
    half = jnp.bfloat16
    dma = pltpu.SemaphoreType.DMA
    anywhere = pl.BlockSpec(memory_space=pl.ANY)
    return pl.pallas_call(
        functools.partial(exchange, outer, lanes_y),
        out_shape=(
            jax.ShapeDtypeStruct((2, lanes_y, frames) + tile, half),
            jax.ShapeDtypeStruct((2, lanes_y, HALO) + tile, half),
            jax.ShapeDtypeStruct((2, 2 * outer) + padded, half),
            jax.ShapeDtypeStruct((HALO,) + queries.shape[1:], half),
        ),
        in_specs=[anywhere] * 4,
        out_specs=(anywhere,) * 4,
        scratch_shapes=[
            pltpu.VMEM(keys.shape, half),
            pltpu.VMEM(values.shape, half),
            pltpu.VMEM(weight.shape, half),
            pltpu.VMEM((2,) + padded, half),
            pltpu.VMEM((2, lanes_y, frames) + tile, half),
            pltpu.VMEM((lanes_y, frames) + tile, half),
            pltpu.VMEM((lanes_y, frames) + tile, half),
            pltpu.VMEM((lanes_y, frames) + tile, half),
            pltpu.VMEM((frames,) + tile, jnp.float32),
            pltpu.VMEM((frames,) + tile, half),
            pltpu.VMEM((HALO,) + tile, half),
            pltpu.VMEM((2, HALO) + tile, half),
            pltpu.VMEM(tile, half),
            pltpu.VMEM(tile, half),
            pltpu.VMEM((outer,) + tile, half),
            pltpu.VMEM(tile, half),
            pltpu.VMEM(queries.shape[1:], half),
            dma((6,)),
            dma((3 + 3 * lanes_y, 2)),
            dma((2, outer, 2)),
            dma((count, 2)),
            dma((count, lanes_y, 2)),
            dma((count, 2)),
            dma((count, 2)),
            dma((count, lanes_y, 2)),
            dma((HALO + 5 + outer, 2)),
        ],
        compiler_params=pltpu.CompilerParams(
            collective_id=0, has_side_effects=True, vmem_limit_bytes=56 * 2**20),
    )(keys, values, weight, queries)


def project(deep, q_hbm, early_hbm, cum_hbm, pre_hbm, w_hbm, taps_ref, out_ref,
            q_ref, early_ref, cum_ref, pre_ref, w_ref, head_ref, att_ref, sems):
    frames, width, tokens = q_ref.shape
    lanes_y, rows = cum_ref.shape[1], cum_ref.shape[3]
    sections, deep_pad, half = w_hbm.shape[1:]
    moves = [(q_hbm, q_ref), (early_hbm, early_ref), (pre_hbm, pre_ref), (cum_hbm, cum_ref),
             (w_hbm.at[0], w_ref.at[0]), (w_hbm.at[1], w_ref.at[1])]
    loads = [pltpu.make_async_copy(src, dst, sems.at[n]) for n, (src, dst) in enumerate(moves)]
    for load in loads:
        load.start()
    gap = jnp.zeros((LANES - HEAD_DIM, tokens), jnp.bfloat16)
    head_ref[...] = jnp.zeros(head_ref.shape, jnp.bfloat16)

    def place(channel):
        section, at = channel // deep, channel % deep
        return section * deep_pad + section * deep % 16 + at

    def state(ref, f, h):
        pieces = [ref[(p // rows) // lanes_y, (p // rows) % lanes_y, f, p % rows:p % rows + e - p]
                  for p, e in cuts(h * LANES, (h + 1) * LANES, rows)]
        return pieces[0] if len(pieces) == 1 else jnp.concatenate(pieces, axis=0)

    def attend(f, query, states):
        for h in range(HEADS):
            low, high = h * HEAD_DIM, (h + 1) * HEAD_DIM
            rows_in = jnp.maximum(query(low, high), 0)
            terms = states(h)
            sums = jnp.dot(jnp.concatenate(terms, axis=1),
                           jnp.concatenate([rows_in, gap] * len(terms), axis=0),
                           preferred_element_type=jnp.float32)
            result = sums[:HEAD_DIM] * (1.0 / (sums[HEAD_DIM:HEAD_DIM + 1] + stab_eps))
            pieces, end = [], None
            for p, e in cuts(low, high, deep):
                if end is not None:
                    pieces.append(jnp.zeros((place(p) - end, tokens), jnp.float32))
                pieces.append(result[p - low:e - low])
                end = place(e - 1) + 1
            result = pieces[0] if len(pieces) == 1 else jnp.concatenate(pieces, axis=0)
            head_ref[place(low):end] = result.astype(jnp.bfloat16)
        span = pl.ds(pl.multiple_of(f * tokens, LANES), tokens)
        att_ref[span] = head_ref[...].T

    first = lax.axis_index("frame") == 0
    for load in loads[:3]:
        load.wait()

    @pl.when(first)
    def _():
        att_ref[0:HALO * tokens] = jnp.zeros((HALO * tokens, att_ref.shape[1]), jnp.bfloat16)

    @pl.when(jnp.logical_not(first))
    def _():
        @pl.loop(0, HALO)
        def _(f):
            attend(f, lambda low, high: early_ref[f, low:high], lambda h: [state(pre_ref, f, h)])

    loads[3].wait()

    @pl.loop(0, frames)
    def _(f):
        attend(f + HALO, lambda low, high: q_ref[f, low:high],
               lambda h: [state(pre_ref, 1, h), state(cum_ref, f, h)])

    def columns(weight, start, count):
        result = jnp.dot(att_ref[...], weight, preferred_element_type=jnp.float32)
        result = result.astype(jnp.bfloat16).astype(jnp.float32)
        result = result.reshape(HALO + frames, tokens, weight.shape[1])[:, :, :count]
        span = pl.ds(start, count)
        taps = [taps_ref[n:n + 1, span] for n in range(3)]
        for f in range(frames):
            mixed = taps[0] * result[f + 2] + taps[1] * result[f + 1] + taps[2] * result[f]
            out_ref[f, span] = mixed.T.astype(jnp.bfloat16)

    deepest = sections * deep_pad
    step = 2 * LANES
    whole = half // step
    rest = half - whole * step

    def weight(n, span):
        return w_ref[n, :, :, span].reshape(deepest, span.size)

    loads[4].wait()

    @pl.loop(0, whole)
    def _(t):
        at = pl.multiple_of(t * step, step)
        columns(weight(0, pl.ds(at, step)), at, step)

    loads[5].wait()
    if rest:
        both = jnp.concatenate([weight(0, pl.ds(half - rest, rest)), weight(1, pl.ds(0, rest))], axis=1)
        columns(both, half - rest, 2 * rest)

    @pl.loop(0, whole - 1)
    def _(t):
        at = pl.multiple_of(t * step + rest, LANES)
        columns(weight(1, pl.ds(at, step)), pl.multiple_of(half + at, LANES), step)

    at = (whole - 1) * step + rest
    columns(weight(1, pl.ds(at, step)), half + at, width - half - at)


def projection(queries, earlier, cum, pre, weight, taps, deep):
    frames, width, tokens = queries.shape
    rows = (HALO + frames) * tokens
    depth = weight.shape[1] * weight.shape[2]
    whole = pl.BlockSpec(memory_space=pltpu.VMEM)
    anywhere = pl.BlockSpec(memory_space=pl.ANY)
    return pl.pallas_call(
        functools.partial(project, deep),
        out_shape=jax.ShapeDtypeStruct(queries.shape, queries.dtype),
        in_specs=[anywhere] * 5 + [whole],
        out_specs=whole,
        scratch_shapes=[pltpu.VMEM(ref.shape, ref.dtype) for ref in (queries, earlier, cum, pre, weight)] + [
            pltpu.VMEM((depth, tokens), jnp.bfloat16),
            pltpu.VMEM((rows, depth), jnp.bfloat16),
            pltpu.SemaphoreType.DMA((6,)),
        ],
        cost_estimate=pl.CostEstimate(
            flops=2 * rows * depth * width, bytes_accessed=2 * depth * width, transcendentals=0),
        compiler_params=pltpu.CompilerParams(vmem_limit_bytes=58 * 2**20),
    )(queries, earlier, cum, pre, weight, taps)


def up_to(value, multiple):
    return -(-value // multiple) * multiple


def per_device(sections, lanes, queries, keys, values, out_weight, conv_taps):
    width = queries.shape[2]
    lanes_y, outer = lanes // 2, sections // 2
    queries, keys, values = (jnp.swapaxes(a, 1, 2) for a in (queries, keys, values))
    tall = up_to(HEADS * LANES, 16 * lanes) // lanes
    deep = out_weight.shape[0]
    shift = max(n * deep % 16 for n in range(sections))
    padded = (up_to(deep + shift, 16 * lanes_y), up_to(width, 2 * LANES) // 2)
    cum, pre, weight, earlier = exchanged(
        keys, values, out_weight, queries, padded, tall, outer, lanes_y)
    mixed = projection(queries, earlier, cum, pre, weight, conv_taps, deep)
    return jnp.swapaxes(mixed, 1, 2)


def solution(mesh):
    split = P("frame", "space", None)
    return jax.shard_map(
        functools.partial(per_device, mesh.shape["frame"], mesh.shape["space"]), mesh=mesh,
        in_specs=(split, split, split, P("frame", None), P()), out_specs=split, check_vma=False)
```

```python
import functools

import jax
import jax.numpy as jnp
from jax import lax
from jax.experimental import pallas as pl
from jax.experimental.pallas import tpu as pltpu
from jax.sharding import PartitionSpec as P

HEADS = 20
HEAD_DIM = 112
LANES = 128
HALO = 2
stab_eps = 1e-06
MESH = pl.DeviceIdType.MESH


def cuts(start, stop, size):
    while start < stop:
        end = min(stop, (start // size + 1) * size)
        yield start, end
        start = end


def exchange(outer, lanes_y, k_hbm, v_hbm, w_hbm, q_in, cum_out, pre_out, w_out, q_out,
             k_in, v_in, w_own, w_in, kv_in, sib_kv, chip_kv, y_kv, frame_kv, cum, pre, x_got, pair_msg, edge_msg, pair_got, edge_got, relay,
             own_sem, kv_sem, z_sem, x_sem, y_sem, sz_sem, sx_sem, sy_sem, p_sem):
    frame = lax.axis_index("frame")
    space = lax.axis_index("space")
    o, i = frame // 2, frame % 2
    y, c = space // 2, space % 2
    frames, tall = kv_in.shape[2], kv_in.shape[3]
    rows = w_in.shape[1]
    part = rows // lanes_y

    def at(o_=None, i_=None, y_=None, c_=None):
        o_ = o if o_ is None else o_
        i_ = i if i_ is None else i_
        y_ = y if y_ is None else y_
        c_ = c if c_ is None else c_
        return (o_ * 2 + i_, y_ * 2 + c_)

    def copy(src, dst, sems, to):
        return pltpu.make_async_remote_copy(
            src_ref=src, dst_ref=dst, send_sem=sems.at[0], recv_sem=sems.at[1],
            device_id=to, device_id_type=MESH)

    def when(cond, do):
        if cond is True:
            do()
        else:
            pl.when(cond)(do)

    def y_far(d):
        return lax.rem(y + d, lanes_y)

    def y_from(d):
        return lax.rem(y + lanes_y - d, lanes_y)

    incoming = [pltpu.make_async_copy(src, dst, own_sem.at[3 + n])
                for n, (src, dst) in enumerate(((w_hbm, w_own), (k_hbm, k_in), (v_hbm, v_in)))]
    for load in incoming:
        load.start()

    barrier = pltpu.get_barrier_semaphore()

    def greet(to):
        pl.semaphore_signal(barrier, inc=1, device_id=to, device_id_type=MESH)

    for d in range(1, outer):
        greet(at(o_=lax.rem(o + d, outer)))
    for d in range(1, lanes_y):
        greet(at(y_=y_far(d)))
    greet(at(i_=1 - i))
    greet(at(c_=1 - c))
    deep, width = w_own.shape
    half = w_in.shape[2]
    w_in[...] = jnp.zeros(w_in.shape, jnp.bfloat16)
    incoming[0].wait()
    for shift in sorted({n * deep % 16 for n in range(2 * outer)}):
        def lay(shift=shift):
            w_in[0, shift:shift + deep, :] = w_own[:, :half]
            w_in[1, shift:shift + deep, :width - half] = w_own[:, half:]
        pl.when(lax.rem(frame * deep, 16) == shift)(lay)

    peers = (outer - 1) + (lanes_y - 1) + 2
    pl.semaphore_wait(barrier, peers)

    def source(key):
        t = (key + 1) // 2
        if key == 0:
            return o, True
        if key % 2:
            return o - t, o >= t
        return o + t, o + t < outer

    keys = range(2 * outer - 1)
    sent = []

    def launch(cond, make):
        when(cond, lambda: make().start())
        sent.append((cond, make))

    def mine(key):
        return w_out.at[c, source(key)[0] * 2 + i]

    def theirs(key, y_):
        span = pl.ds(pl.multiple_of(y_ * part, 16), part)
        return w_out.at[c, source(key)[0] * 2 + 1 - i, span]

    def z_copy(up, t):
        g = ((o - t + 1) if up else (o + t - 1)) * 2 + i
        dst = w_out.at[c, g]
        return copy(w_in.at[c] if t == 1 else dst, dst, z_sem.at[0 if up else 1, t],
                    at(o_=o + 1 if up else o - 1))

    def z_send(t):
        launch(jnp.logical_and(o < outer - 1, o - t + 1 >= 0), lambda: z_copy(True, t))
        launch(jnp.logical_and(o > 0, o + t - 1 < outer), lambda: z_copy(False, t))

    def z_wait(t):
        def got(key, up):
            ref = mine(key)
            copy(ref, ref, z_sem.at[0 if up else 1, t], at(c_=1 - c)).wait_recv()
        when(source(2 * t - 1)[1], lambda: got(2 * t - 1, True))
        when(source(2 * t)[1], lambda: got(2 * t, False))

    def x_copy(key):
        span = pl.ds(pl.multiple_of(y * part, 16), part)
        src = w_in.at[c, span] if key == 0 else mine(key).at[span]
        return copy(src, mine(key).at[span], x_sem.at[key], at(i_=1 - i))

    def x_send(key):
        launch(source(key)[1], lambda: x_copy(key))

    def sib_z(key):
        launch(source(key)[1], lambda: copy(mine(key), mine(key), sz_sem.at[key], at(c_=1 - c)))

    def x_pass(key):
        def got():
            ref = theirs(key, y)
            copy(ref, ref, x_sem.at[key], at(i_=1 - i)).wait_recv()
        cond = source(key)[1]
        when(cond, got)
        for d in range(1, lanes_y):
            launch(cond, lambda d=d: copy(theirs(key, y), theirs(key, y), y_sem.at[key, d],
                                          at(y_=y_far(d))))
        launch(cond, lambda: copy(theirs(key, y), theirs(key, y), sx_sem.at[key], at(c_=1 - c)))

    def y_pass(key):
        cond = source(key)[1]
        for d in range(1, lanes_y):
            def got(d=d):
                ref = theirs(key, y_from(d))
                copy(ref, ref, y_sem.at[key, d], at(y_=y_far(d))).wait_recv()
            when(cond, got)
            launch(cond, lambda d=d: copy(theirs(key, y_from(d)), theirs(key, y_from(d)),
                                          sy_sem.at[key, d], at(c_=1 - c)))

    def sib_wait(key):
        cond = source(key)[1]
        g = source(key)[0] * 2

        def got(ref, sems):
            copy(ref, ref, sems, at(c_=1 - c)).wait_recv()
        if key:
            when(cond, lambda: got(w_out.at[1 - c, g + i], sz_sem.at[key]))
        for d in range(lanes_y):
            span = pl.ds(pl.multiple_of(y_from(d) * part, 16), part)
            sems = sx_sem.at[key] if d == 0 else sy_sem.at[key, d]
            when(cond, lambda span=span, sems=sems: got(w_out.at[1 - c, g + 1 - i, span], sems))

    z_send(1)
    x_send(0)
    locals_ = [pltpu.make_async_copy(w_in, w_out.at[:, frame], own_sem.at[0])]
    locals_[0].start()

    via = HALO + 1 + outer
    onward = jnp.logical_and(i == 1, o < outer - 1)
    last = frames - HALO

    def halo_pair(f):
        launch(i == 0, lambda: copy(q_in.at[last + f], q_out.at[f], p_sem.at[f], at(i_=1)))

    def halo_onward():
        launch(onward, lambda: copy(q_in.at[last], relay, p_sem.at[via], at(i_=0)))
        launch(onward, lambda: copy(q_in.at[last + 1], relay, p_sem.at[via + 1], at(o_=o + 1)))

    def halo_pass():
        lower = jnp.logical_and(i == 0, o < outer - 1)
        upper = jnp.logical_and(i == 1, o > 0)
        when(lower, lambda: copy(relay, relay, p_sem.at[via], at(c_=1 - c)).wait_recv())
        launch(lower, lambda: copy(relay, q_out.at[0], p_sem.at[via + 2], at(o_=o + 1)))
        when(upper, lambda: copy(relay, relay, p_sem.at[via + 1], at(c_=1 - c)).wait_recv())
        launch(upper, lambda: copy(relay, q_out.at[1], p_sem.at[via + 3], at(i_=0)))

    for load in incoming[1:]:
        load.wait()

    tokens = k_in.shape[2]
    gap = LANES - HEAD_DIM
    nothing = jnp.zeros((gap, tokens), jnp.bfloat16)
    ones = jnp.ones((gap, tokens), jnp.bfloat16)

    @pl.loop(0, frames)
    def _(f):
        for h in range(HEADS):
            span = slice(h * HEAD_DIM, (h + 1) * HEAD_DIM)
            key = jnp.concatenate([jnp.maximum(k_in[f, span], 0), nothing], axis=0)
            value = jnp.concatenate([v_in[f, span], ones], axis=0)
            sums = lax.dot_general(value, key, (((1,), (1,)), ((), ())),
                                   preferred_element_type=jnp.float32).astype(jnp.bfloat16)
            for p, e in cuts(h * LANES, (h + 1) * LANES, tall):
                n = p // tall
                kv_in[n // lanes_y, n % lanes_y, f, p % tall:p % tall + e - p] = (
                    sums[p - h * LANES:e - h * LANES])

    sib_copy = copy(kv_in.at[1 - c], sib_kv, kv_sem.at[0], at(c_=1 - c))
    sib_copy.start()
    sib_copy.wait_recv()
    for d in list(range(1, lanes_y)) + [0]:
        to = y_far(d)
        for f in range(frames):
            chip_kv[to, f] = (kv_in[c, to, f].astype(jnp.float32)
                              + sib_kv[to, f].astype(jnp.float32)).astype(jnp.bfloat16)
        if d:
            launch(True, lambda d=d: copy(chip_kv.at[y_far(d)], y_kv.at[d], kv_sem.at[3 + d],
                                          at(y_=y_far(d))))
    halo_pair(0)
    halo_onward()
    z_wait(1)
    if outer > 2:
        z_send(2)
    for key in (1, 2):
        x_send(key)
        sib_z(key)
    for d in range(1, lanes_y):
        copy(chip_kv.at[y_far(d)], y_kv.at[d], kv_sem.at[3 + d], at(y_=y_far(d))).wait_recv()
    for f in range(frames):
        total = chip_kv[y, f].astype(jnp.float32)
        for d in range(1, lanes_y):
            total = total + y_kv[d, f].astype(jnp.float32)
        frame_kv[f] = total if f == 0 else frame_kv[f - 1] + total
    for f in range(HALO):
        x_got[0, f] = frame_kv[frames - 1 - f].astype(jnp.bfloat16)
    launch(True, lambda: copy(x_got.at[0], x_got.at[1], p_sem.at[HALO], at(i_=1 - i)))
    for f in range(frames):
        cum[f] = frame_kv[f].astype(jnp.bfloat16)
    for d in range(1, lanes_y):
        launch(True, lambda d=d: copy(cum, cum_out.at[c, y], kv_sem.at[3 + lanes_y + d], at(y_=y_far(d))))
    locals_.append(pltpu.make_async_copy(cum, cum_out.at[c, y], own_sem.at[1]))
    locals_[1].start()
    x_pass(0)

    def pair():
        copy(x_got.at[0], x_got.at[1], p_sem.at[HALO], at(i_=1 - i)).wait_recv()
        pair_msg[...] = (x_got[0, 0].astype(jnp.float32) + x_got[1, 0].astype(jnp.float32)).astype(jnp.bfloat16)
        low = jnp.where(i == 0, x_got[0, 0].astype(jnp.float32), x_got[1, 0].astype(jnp.float32))
        high = jnp.where(i == 0, x_got[1, 1].astype(jnp.float32), x_got[0, 1].astype(jnp.float32))
        edge_msg[...] = (low + high).astype(jnp.bfloat16)
        for d in range(1, outer):
            launch(o + d < outer,
                   lambda d=d: copy(pair_msg, pair_got.at[d], p_sem.at[HALO + 1 + d], at(o_=o + d)))
        launch(jnp.logical_and(i == 0, o + 1 < outer), lambda: copy(edge_msg, edge_got, p_sem.at[HALO + 1], at(o_=o + 1)))

    def prefix():
        for d in range(1, outer):
            when(o >= d, lambda d=d: copy(pair_msg, pair_got.at[d], p_sem.at[HALO + 1 + d],
                                          at(c_=1 - c)).wait_recv())
        when(jnp.logical_and(i == 0, o >= 1), lambda: copy(edge_msg, edge_got, p_sem.at[HALO + 1], at(c_=1 - c)).wait_recv())
        zero = jnp.zeros(pair_msg.shape, jnp.float32)
        far = zero
        for d in range(2, outer):
            far = far + jnp.where(o >= d, pair_got[d].astype(jnp.float32), zero)
        near = jnp.where(o >= 1, pair_got[1].astype(jnp.float32), zero)
        edge = jnp.where(o >= 1, edge_got[...].astype(jnp.float32), zero)
        base = far + near
        before = jnp.where(i == 0, base, base + x_got[1, 0].astype(jnp.float32))
        second = jnp.where(i == 0, far + edge, base + x_got[1, 1].astype(jnp.float32))
        pre[0] = second.astype(jnp.bfloat16)
        pre[1] = before.astype(jnp.bfloat16)
        for d in range(1, lanes_y):
            launch(True, lambda d=d: copy(pre, pre_out.at[c, y], kv_sem.at[3 + 2 * lanes_y + d],
                                          at(y_=y_far(d))))
        locals_.append(pltpu.make_async_copy(pre, pre_out.at[c, y], own_sem.at[2]))
        locals_[2].start()

    def hand_on(out, first, own, sems):
        for d in range(1, lanes_y):
            ref = out.at[c, y_from(d)]
            copy(ref, ref, kv_sem.at[first + d], at(y_=y_far(d))).wait_recv()
        own.wait()
        launch(True, lambda: copy(out.at[c], out.at[c], sems, at(c_=1 - c)))

    for t in range(2, outer):
        z_wait(t)
        if t + 1 < outer:
            z_send(t + 1)
        for key in (2 * t - 1, 2 * t):
            x_send(key)
            sib_z(key)
        if t == 2:
            pair()
            halo_pair(1)
        for key in (2 * t - 3, 2 * t - 2):
            x_pass(key)
        if t == 2:
            halo_pass()
        for key in ((0,) if t == 2 else (2 * t - 5, 2 * t - 4)):
            y_pass(key)
    if outer <= 2:
        pair()
        halo_pair(1)
        halo_pass()
        y_pass(0)
    prefix()
    if outer > 2:
        for key in (2 * outer - 5, 2 * outer - 4):
            y_pass(key)
    hand_on(cum_out, 3 + lanes_y, locals_[1], kv_sem.at[1])
    for key in (2 * outer - 3, 2 * outer - 2):
        x_pass(key)
    hand_on(pre_out, 3 + 2 * lanes_y, locals_[2], kv_sem.at[2])
    for key in (2 * outer - 3, 2 * outer - 2):
        y_pass(key)

    for out, sems in ((cum_out, kv_sem.at[1]), (pre_out, kv_sem.at[2])):
        other = out.at[1 - c]
        copy(other, other, sems, at(c_=1 - c)).wait_recv()
    for f in range(HALO):
        def landed(sems, f):
            copy(q_out.at[f], q_out.at[f], sems, at(c_=1 - c)).wait_recv()
        when(i == 1, lambda f=f: landed(p_sem.at[f], f))
        when(jnp.logical_and(i == 0, o > 0), lambda f=f: landed(p_sem.at[via + 2 + f], f))
    for key in keys:
        sib_wait(key)
    locals_[0].wait()
    sib_copy.wait_send()
    for cond, make in sent:
        when(cond, lambda make=make: make().wait_send())


def exchanged(keys, values, weight, queries, padded, tall, outer, lanes_y):
    frames = keys.shape[0]
    count = 2 * outer - 1
    tile = (tall, LANES)
    half = jnp.bfloat16
    dma = pltpu.SemaphoreType.DMA
    anywhere = pl.BlockSpec(memory_space=pl.ANY)
    return pl.pallas_call(
        functools.partial(exchange, outer, lanes_y),
        out_shape=(
            jax.ShapeDtypeStruct((2, lanes_y, frames) + tile, half),
            jax.ShapeDtypeStruct((2, lanes_y, HALO) + tile, half),
            jax.ShapeDtypeStruct((2, 2 * outer) + padded, half),
            jax.ShapeDtypeStruct((HALO,) + queries.shape[1:], half),
        ),
        in_specs=[anywhere] * 4,
        out_specs=(anywhere,) * 4,
        scratch_shapes=[
            pltpu.VMEM(keys.shape, half),
            pltpu.VMEM(values.shape, half),
            pltpu.VMEM(weight.shape, half),
            pltpu.VMEM((2,) + padded, half),
            pltpu.VMEM((2, lanes_y, frames) + tile, half),
            pltpu.VMEM((lanes_y, frames) + tile, half),
            pltpu.VMEM((lanes_y, frames) + tile, half),
            pltpu.VMEM((lanes_y, frames) + tile, half),
            pltpu.VMEM((frames,) + tile, jnp.float32),
            pltpu.VMEM((frames,) + tile, half),
            pltpu.VMEM((HALO,) + tile, half),
            pltpu.VMEM((2, HALO) + tile, half),
            pltpu.VMEM(tile, half),
            pltpu.VMEM(tile, half),
            pltpu.VMEM((outer,) + tile, half),
            pltpu.VMEM(tile, half),
            pltpu.VMEM(queries.shape[1:], half),
            dma((6,)),
            dma((3 + 3 * lanes_y, 2)),
            dma((2, outer, 2)),
            dma((count, 2)),
            dma((count, lanes_y, 2)),
            dma((count, 2)),
            dma((count, 2)),
            dma((count, lanes_y, 2)),
            dma((HALO + 5 + outer, 2)),
        ],
        compiler_params=pltpu.CompilerParams(
            collective_id=0, has_side_effects=True, vmem_limit_bytes=56 * 2**20),
    )(keys, values, weight, queries)


def project(deep, q_hbm, early_hbm, cum_hbm, pre_hbm, w_hbm, taps_ref, out_ref,
            q_ref, early_ref, cum_ref, pre_ref, w_ref, head_ref, att_ref, sems):
    frames, width, tokens = q_ref.shape
    lanes_y, rows = cum_ref.shape[1], cum_ref.shape[3]
    sections, deep_pad, half = w_hbm.shape[1:]
    moves = [(q_hbm, q_ref), (early_hbm, early_ref), (pre_hbm, pre_ref), (cum_hbm, cum_ref),
             (w_hbm.at[0], w_ref.at[0]), (w_hbm.at[1], w_ref.at[1])]
    loads = [pltpu.make_async_copy(src, dst, sems.at[n]) for n, (src, dst) in enumerate(moves)]
    for load in loads:
        load.start()
    gap = jnp.zeros((LANES - HEAD_DIM, tokens), jnp.bfloat16)
    head_ref[...] = jnp.zeros(head_ref.shape, jnp.bfloat16)

    def place(channel):
        section, at = channel // deep, channel % deep
        return section * deep_pad + section * deep % 16 + at

    def state(ref, f, h):
        pieces = [ref[(p // rows) // lanes_y, (p // rows) % lanes_y, f, p % rows:p % rows + e - p]
                  for p, e in cuts(h * LANES, (h + 1) * LANES, rows)]
        return pieces[0] if len(pieces) == 1 else jnp.concatenate(pieces, axis=0)

    def attend(f, query, states):
        for h in range(HEADS):
            low, high = h * HEAD_DIM, (h + 1) * HEAD_DIM
            rows_in = jnp.maximum(query(low, high), 0)
            terms = states(h)
            sums = jnp.dot(jnp.concatenate(terms, axis=1),
                           jnp.concatenate([rows_in, gap] * len(terms), axis=0),
                           preferred_element_type=jnp.float32)
            result = sums[:HEAD_DIM] * (1.0 / (sums[HEAD_DIM:HEAD_DIM + 1] + stab_eps))
            pieces, end = [], None
            for p, e in cuts(low, high, deep):
                if end is not None:
                    pieces.append(jnp.zeros((place(p) - end, tokens), jnp.float32))
                pieces.append(result[p - low:e - low])
                end = place(e - 1) + 1
            result = pieces[0] if len(pieces) == 1 else jnp.concatenate(pieces, axis=0)
            head_ref[place(low):end] = result.astype(jnp.bfloat16)
        span = pl.ds(pl.multiple_of(f * tokens, LANES), tokens)
        att_ref[span] = head_ref[...].T

    first = lax.axis_index("frame") == 0
    for load in loads[:3]:
        load.wait()

    @pl.when(first)
    def _():
        att_ref[0:HALO * tokens] = jnp.zeros((HALO * tokens, att_ref.shape[1]), jnp.bfloat16)

    @pl.when(jnp.logical_not(first))
    def _():
        @pl.loop(0, HALO)
        def _(f):
            attend(f, lambda low, high: early_ref[f, low:high], lambda h: [state(pre_ref, f, h)])

    loads[3].wait()

    @pl.loop(0, frames)
    def _(f):
        attend(f + HALO, lambda low, high: q_ref[f, low:high],
               lambda h: [state(pre_ref, 1, h), state(cum_ref, f, h)])

    def columns(weight, start, count):
        result = jnp.dot(att_ref[...], weight, preferred_element_type=jnp.float32)
        result = result.astype(jnp.bfloat16).astype(jnp.float32)
        result = result.reshape(HALO + frames, tokens, weight.shape[1])[:, :, :count]
        span = pl.ds(start, count)
        taps = [taps_ref[n:n + 1, span] for n in range(3)]
        for f in range(frames):
            mixed = taps[0] * result[f + 2] + taps[1] * result[f + 1] + taps[2] * result[f]
            out_ref[f, span] = mixed.T.astype(jnp.bfloat16)

    deepest = sections * deep_pad
    step = 2 * LANES
    whole = half // step
    rest = half - whole * step

    def weight(n, span):
        return w_ref[n, :, :, span].reshape(deepest, span.size)

    loads[4].wait()

    @pl.loop(0, whole)
    def _(t):
        at = pl.multiple_of(t * step, step)
        columns(weight(0, pl.ds(at, step)), at, step)

    loads[5].wait()
    if rest:
        both = jnp.concatenate([weight(0, pl.ds(half - rest, rest)), weight(1, pl.ds(0, rest))], axis=1)
        columns(both, half - rest, 2 * rest)

    @pl.loop(0, whole - 1)
    def _(t):
        at = pl.multiple_of(t * step + rest, LANES)
        columns(weight(1, pl.ds(at, step)), pl.multiple_of(half + at, LANES), step)

    at = (whole - 1) * step + rest
    columns(weight(1, pl.ds(at, step)), half + at, width - half - at)


def projection(queries, earlier, cum, pre, weight, taps, deep):
    frames, width, tokens = queries.shape
    rows = (HALO + frames) * tokens
    depth = weight.shape[1] * weight.shape[2]
    whole = pl.BlockSpec(memory_space=pltpu.VMEM)
    anywhere = pl.BlockSpec(memory_space=pl.ANY)
    return pl.pallas_call(
        functools.partial(project, deep),
        out_shape=jax.ShapeDtypeStruct(queries.shape, queries.dtype),
        in_specs=[anywhere] * 5 + [whole],
        out_specs=whole,
        scratch_shapes=[pltpu.VMEM(ref.shape, ref.dtype) for ref in (queries, earlier, cum, pre, weight)] + [
            pltpu.VMEM((depth, tokens), jnp.bfloat16),
            pltpu.VMEM((rows, depth), jnp.bfloat16),
            pltpu.SemaphoreType.DMA((6,)),
        ],
        cost_estimate=pl.CostEstimate(
            flops=2 * rows * depth * width, bytes_accessed=2 * depth * width, transcendentals=0),
        compiler_params=pltpu.CompilerParams(vmem_limit_bytes=58 * 2**20),
    )(queries, earlier, cum, pre, weight, taps)


def up_to(value, multiple):
    return -(-value // multiple) * multiple


def per_device(sections, lanes, queries, keys, values, out_weight, conv_taps):
    width = queries.shape[2]
    lanes_y, outer = lanes // 2, sections // 2
    queries, keys, values = (jnp.swapaxes(a, 1, 2) for a in (queries, keys, values))
    tall = up_to(HEADS * LANES, 16 * lanes) // lanes
    deep = out_weight.shape[0]
    shift = max(n * deep % 16 for n in range(sections))
    padded = (up_to(deep + shift, 16 * lanes_y), up_to(width, 2 * LANES) // 2)
    cum, pre, weight, earlier = exchanged(
        keys, values, out_weight, queries, padded, tall, outer, lanes_y)
    mixed = projection(queries, earlier, cum, pre, weight, conv_taps, deep)
    return jnp.swapaxes(mixed, 1, 2)


def solution(mesh):
    split = P("frame", "space", None)
    return jax.shard_map(
        functools.partial(per_device, mesh.shape["frame"], mesh.shape["space"]), mesh=mesh,
        in_specs=(split, split, split, P("frame", None), P()), out_specs=split, check_vma=False)
```
